128 devices in a mesh: frame: 2 (over y_hi), plane: 64 (over z, y_lo, x, core).
Axes of the slice: x: 4, y: 4 (y_hi: 2, y_lo: 2; y = y_hi * 2 + y_lo), z: 4, core: 2. Of those that a mesh axis runs over, the one named last changes fastest.
Arguments:
- states: float32 [4, 2, 64, 256, 256], P(None, 'frame', 'plane'), may hold values from -6 to 6
- measured: float32 [2, 64, 256, 256], P('frame', 'plane'), may hold values from -6 to 6
- response: float32 [256, 256], replicated, may hold values from 0.1 to 10
- kernel_in: bfloat16 [3, 9, 32, 2], replicated, may hold values from -1.5 to 1.5
- bias_in: float32 [3, 32], replicated, may hold values from -3 to 3
- kernel_mid: bfloat16 [3, 1, 9, 32, 32], replicated, may hold values from -0.375 to 0.375
- bias_mid: float32 [3, 1, 32], replicated, may hold values from -3 to 3
- kernel_out: bfloat16 [3, 9, 32], replicated, may hold values from -0.375 to 0.375
Outputs:
- new_states: float32 [4, 2, 64, 256, 256], P(None, 'frame', 'plane')
The draws below stay inside these ranges and needn't reach their ends.
All inputs are finite; a program needn't handle non-finite values.
Results may differ from the reference program's by a relative error of at most 0.0056.
Values may be sent and summed in bfloat16 or wider, within the bound.
A program may use at most 192 MiB of HBM per device.

```python
import math
import jax
import jax.numpy as jnp
from jax import lax

N = 256
C = 32
LAYERS = 3
Z = 64


def levels(stream_key, dims, shards, low, top_value):
    def one(axis_at, parts):
        heights = jax.random.uniform(jax.random.fold_in(jax.random.fold_in(stream_key, 6), axis_at), (parts,), jnp.float32, low / len(shards), top_value / len(shards))
        return jnp.repeat(jnp.exp(heights), dims[axis_at] // parts).reshape((-1,) + (1,) * (len(dims) - axis_at - 1))

    loudness = one(*shards[0])
    for cut in shards[1:]:
        loudness = loudness * one(*cut)
    return loudness


def centred(stream_key, shape, scale, reach, shards=(), kind=jnp.bfloat16):
    drawn = scale * jax.random.normal(stream_key, shape, jnp.float32)
    if shards:
        drawn = drawn * levels(stream_key, shape, shards, -0.22, 0.18)
    return jnp.clip(drawn, -reach, reach).astype(kind)


def setup_inputs(seed: int = 0) -> dict:
    seeds = jax.random.split(jax.random.key(seed), 9)
    return {
        "states": centred(seeds[0], (4, 2, Z, N, N), 1.0, 6.0, ((1, 2), (2, 64)), jnp.float32),
        "measured": centred(seeds[1], (2, Z, N, N), 1.0, 6.0, ((0, 2), (1, 64)), jnp.float32),
        "response": jnp.clip(jnp.exp(jax.random.uniform(seeds[2], (N, N), jnp.float32, math.log(0.1), math.log(10.0))), 0.1, 10.0),
        "kernel_in": centred(seeds[3], (3, 9, C, 2), 18 ** -0.5, 1.5),
        "bias_in": centred(seeds[4], (3, C), 0.5, 3.0, (), jnp.float32),
        "kernel_mid": centred(seeds[5], (3, LAYERS - 2, 9, C, C), (9 * C) ** -0.5, 0.375),
        "bias_mid": centred(seeds[6], (3, LAYERS - 2, C), 0.5, 3.0, (), jnp.float32),
        "kernel_out": centred(seeds[7], (3, 9, C), (9 * C) ** -0.5, 0.375),
    }


relaxation = 0.8


def fourier_tables(length):
    indices = jnp.arange(length, dtype=jnp.int32)
    phase = (indices[:, None] * indices[None, :]) % length
    angle = phase.astype(jnp.float32) * (2.0 * math.pi / length)
    return jnp.cos(angle).astype(jnp.bfloat16), jnp.sin(angle).astype(jnp.bfloat16)


def along_last(values, table):
    return jnp.einsum("pyx,kx->pyk", values.astype(jnp.float32), table.astype(jnp.float32), precision=lax.Precision.HIGHEST)


def along_middle(table, values):
    return jnp.einsum("ky,pyx->pkx", table.astype(jnp.float32), values.astype(jnp.float32), precision=lax.Precision.HIGHEST)


def fidelity(volume, filter_gain):
    length = volume.shape[2]
    cosine, sines = fourier_tables(length)
    source = volume.astype(jnp.bfloat16)
    row_real = along_last(source, cosine).astype(jnp.bfloat16)
    row_imag = (-along_last(source, sines)).astype(jnp.bfloat16)
    spec_real = ((along_middle(cosine, row_real) + along_middle(sines, row_imag)) * filter_gain).astype(jnp.bfloat16)
    spec_imag = ((along_middle(cosine, row_imag) - along_middle(sines, row_real)) * filter_gain).astype(jnp.bfloat16)
    back_real = (along_middle(cosine, spec_real) - along_middle(sines, spec_imag)).astype(jnp.bfloat16)
    back_imag = (along_middle(cosine, spec_imag) + along_middle(sines, spec_real)).astype(jnp.bfloat16)
    spatial = along_last(back_real, cosine) - along_last(back_imag, sines)
    return spatial * (1.0 / (length * length))


def convolve(planes_in, kernel):
    rows_count = planes_in.shape[1]
    cols_count = planes_in.shape[2]
    padded = jnp.pad(planes_in, ((0, 0), (1, 1), (1, 1))).astype(jnp.float32)
    summed = jnp.zeros((kernel.shape[1], rows_count, cols_count), jnp.float32)
    for tap_index in range(9):
        row_shift = tap_index // 3
        col_shift = tap_index % 3
        shifted = padded[:, row_shift:row_shift + rows_count, col_shift:col_shift + cols_count]
        summed = summed + jnp.einsum("oc,cab->oab", kernel[tap_index].astype(jnp.float32), shifted)
    return summed


def denoise(channels, which, kernel_in, bias_in, kernel_mid, bias_mid, kernel_out):
    def single_plane(planes_in):
        hidden = jax.nn.relu(convolve(planes_in, kernel_in[which]) + bias_in[which][:, None, None]).astype(jnp.bfloat16)
        for section in range(kernel_mid.shape[1]):
            hidden = jax.nn.relu(convolve(hidden, kernel_mid[which, section]) + bias_mid[which, section][:, None, None]).astype(jnp.bfloat16)
        return convolve(hidden, kernel_out[which][:, None, :])[0].astype(jnp.bfloat16)
    return lax.map(single_plane, channels)


def reference(states, measured, response, kernel_in, bias_in, kernel_mid, bias_mid, kernel_out):
    filter_gain = 1.0 / (1.0 + response)
    rounded = states.astype(jnp.bfloat16)
    results = []
    for frame_index in range(2):
        other = 1 - frame_index
        current = states[:, frame_index]
        data_estimate = fidelity(measured[frame_index] + current[0], filter_gain)
        channels_z = jnp.stack([rounded[1, frame_index], rounded[1, other]], 1)
        residual_z = denoise(channels_z, 0, kernel_in, bias_in, kernel_mid, bias_mid, kernel_out)
        channels_x = jnp.stack([jnp.transpose(rounded[2, frame_index], (2, 0, 1)), jnp.transpose(rounded[2, other], (2, 0, 1))], 1)
        residual_x = jnp.transpose(denoise(channels_x, 1, kernel_in, bias_in, kernel_mid, bias_mid, kernel_out), (1, 2, 0))
        channels_y = jnp.stack([jnp.transpose(rounded[3, frame_index], (1, 0, 2)), jnp.transpose(rounded[3, other], (1, 0, 2))], 1)
        residual_y = jnp.transpose(denoise(channels_y, 2, kernel_in, bias_in, kernel_mid, bias_mid, kernel_out), (1, 0, 2))
        estimates = jnp.stack([
            data_estimate,
            current[1] - residual_z.astype(jnp.float32),
            current[2] - residual_x.astype(jnp.float32),
            current[3] - residual_y.astype(jnp.float32)])
        reflected = 2.0 * estimates - current
        average = jnp.mean(reflected, axis=0)
        results.append((1.0 - relaxation) * current + relaxation * (2.0 * average - reflected))
    return jnp.stack(results, 1)
```

```python
import functools
import math

import jax
import jax.numpy as jnp
import numpy as np
from jax import lax
from jax.experimental import pallas as pl
from jax.experimental.pallas import tpu as pltpu
from jax.sharding import PartitionSpec as P

relaxation = 0.8

GROUPS = [(0, 0), (0, 1), (3, 0), (3, 1), (1, 0), (1, 1), (2, 0), (2, 1)]
STRIP = 16


def block_order(width):
    blocks = width // 2
    per = blocks // STRIP
    lane = np.arange(blocks)
    return (lane % STRIP) * per + lane // STRIP


def spread_table(width):
    blocks = width // 2
    order = block_order(width)
    table = np.zeros((width, 4 * blocks), np.float32)
    for xo in range(4):
        for lane in range(blocks):
            col = 2 * order[lane] + xo - 1
            if 0 <= col < width:
                table[col, xo * blocks + lane] = 1
    return table


def gather_table(width):
    blocks = width // 2
    order = block_order(width)
    table = np.zeros((width, width), np.float32)
    for j in range(2):
        for lane in range(blocks):
            table[j * blocks + lane, 2 * order[lane] + j] = 1
    return table


def select_in():
    chosen = np.zeros((9, 4, 24, 2, 8), np.float32)
    for half in range(2):
        for g, (i, j) in enumerate(GROUPS):
            for p in range(3):
                for q in range(3):
                    chosen[3 * p + q, j + q, 7 + 4 * half + i + p, half, g] = 1
    return chosen.reshape(9, 96, 16)


def slots_mid():
    slots = list(GROUPS)
    slots += [(i, -1 if j == 1 else 2) for i, j in GROUPS]
    slots += [(-1 if i == 3 else 4, j) for i, j in GROUPS[:4]]
    slots += [(-1 if i == 3 else 4, -1 if j == 1 else 2) for i, j in GROUPS[:4]]
    return slots


def select_mid():
    chosen = np.zeros((9, 24, 8), np.float32)
    for s, (row, col) in enumerate(slots_mid()):
        for g, (i, j) in enumerate(GROUPS):
            p, q = row - i + 1, col - j + 1
            if 0 <= p < 3 and 0 <= q < 3:
                chosen[3 * p + q, s, g] = 1
    return chosen


def select_out():
    targets = [None] * 32
    for j in range(2):
        far = 2 if j == 0 else -1
        for i in range(4):
            targets[j * 4 + i] = (i, j)
            targets[8 + j * 4 + i] = (i, far)
        for base, col in ((16, j), (24, far)):
            targets[base + j * 4] = (4, col)
            targets[base + j * 4 + 3] = (-1, col)
    chosen = np.zeros((9, 32, 8), np.float32)
    for r, target in enumerate(targets):
        if target is None:
            continue
        for g, (i, j) in enumerate(GROUPS):
            p, q = i - target[0] + 1, j - target[1] + 1
            if 0 <= p < 3 and 0 <= q < 3:
                chosen[3 * p + q, r, g] = 1
    return chosen


def banded(kernel_in, bias_in, kernel_mid, bias_mid, kernel_out):
    kind = jnp.bfloat16
    d, _, channels, _ = kernel_in.shape
    first = jnp.einsum("tsg,dtoc->dcsgo", select_in().astype(kind), kernel_in, preferred_element_type=kind)
    first = first.reshape(d, 192, 16 * channels)
    mid = jnp.einsum("tsg,dtoc->dscgo", select_mid().astype(kind), kernel_mid[:, 0], preferred_element_type=kind)
    mid = mid.reshape(d, 24 * channels, 8 * channels)
    last = jnp.einsum("trg,dtc->drgc", select_out().astype(kind), kernel_out, preferred_element_type=kind)
    last = last.reshape(d, 32, 8 * channels)
    bias_first = jnp.tile(bias_in[:, None], (1, 1, 16))
    bias_second = jnp.tile(bias_mid[:, 0][:, None], (1, 1, 8))
    return first, bias_first, mid, bias_second, last


def mm(a, b, dims=((1,), (0,))):
    return lax.dot_general(a, b, (dims, ((), ())), preferred_element_type=jnp.float32)


def denoise(x, w_first, b_first, w_mid, b_mid, w_last, spread, gather, emit, u_ref, h_ref, c_ref, d_ref, frames):
    rows = u_ref.shape[1] - 16
    row_blocks = rows // 4
    kind = jnp.bfloat16
    for pair in range(len(x)):
        for ch in range(2):
            u_ref[pair * 2 + ch, :8, :] = jnp.zeros((8, 512), jnp.float32)
            u_ref[pair * 2 + ch, rows + 8:, :] = jnp.zeros((8, 512), jnp.float32)
            u_ref[pair * 2 + ch, 8:rows + 8, :] = mm(x[pair][ch](), spread)
    for img in range(len(x) * frames):
        h_ref[img, 0] = jnp.zeros((160, 256), kind)
        h_ref[img, row_blocks + 1] = jnp.zeros((160, 256), kind)

    first_row = lax.broadcasted_iota(jnp.int32, (16, 256), 0) == 0
    last_row = lax.broadcasted_iota(jnp.int32, (16, 256), 0) == 15

    def first_layer(k, carry):
        start = pl.multiple_of(k * 8, 8)
        for pair in range(len(x)):
            parts = [
                u_ref[pair * 2 + ch, pl.ds(start, 24), xo * 128:(xo + 1) * 128]
                for ch in range(2) for xo in range(4)
            ]
            for f in range(frames):
                ordered = parts if f == 0 else parts[4:] + parts[:4]
                stacked = jnp.concatenate(ordered, 0).astype(kind)
                made = mm(stacked, w_first[...], ((0,), (0,)))
                made = jnp.maximum(made + b_first[...], 0.0)
                for half in range(2):
                    piece = made[:, half * 256:(half + 1) * 256]
                    at = 2 * k + half + 1
                    img = pair * frames + f
                    h_ref[img, at, 16:144, :] = piece.astype(kind)
                    h_ref[img, at, 0:16, :] = jnp.where(first_row, 0.0, pltpu.roll(piece[112:128], 1, 0)).astype(kind)
                    h_ref[img, at, 144:160, :] = jnp.where(last_row, 0.0, pltpu.roll(piece[0:16], 15, 0)).astype(kind)
        return carry

    lax.fori_loop(0, rows // 8, first_layer, 0)

    right = (lax.broadcasted_iota(jnp.int32, (128, 256), 1) // 32) % 2 == 1
    right_half = right[:, :128]
    low = lax.broadcasted_iota(jnp.int32, (128, 128), 1) >= 64

    for img in range(len(x) * frames):

        def mid_layer(a, carry):
            here = h_ref[img, a + 1, 16:144, :]
            side = jnp.where(right, h_ref[img, a + 1, 0:128, :], h_ref[img, a + 1, 32:160, :])
            across = jnp.where(low, h_ref[img, a, 16:144, 0:128], h_ref[img, a + 2, 16:144, 0:128])
            corner_left = jnp.where(low, h_ref[img, a, 0:128, 0:128], h_ref[img, a + 2, 0:128, 0:128])
            corner_right = jnp.where(low, h_ref[img, a, 32:160, 0:128], h_ref[img, a + 2, 32:160, 0:128])
            corner = jnp.where(right_half, corner_left, corner_right)
            made = mm(jnp.concatenate([here, side, across, corner], 1), w_mid[...])
            hidden = jnp.maximum(made + b_mid[...], 0.0).astype(kind)
            c_ref[img, a + 1] = mm(w_last[...], hidden, ((1,), (1,)))
            return carry

        lax.fori_loop(0, row_blocks, mid_layer, 0, unroll=2)

    lane = lax.broadcasted_iota(jnp.int32, (8, 128), 1)
    sub = lax.broadcasted_iota(jnp.int32, (8, 128), 0)

    def moved(value):
        before = jnp.where(lane >= 16, pltpu.roll(value, 16, 1), jnp.where(lane >= 1, pltpu.roll(value, 17, 1), 0.0))
        after = jnp.where(lane < 112, pltpu.roll(value, 112, 1), jnp.where(lane < 127, pltpu.roll(value, 111, 1), 0.0))
        return jnp.where(sub < 4, before, after)

    for img in range(len(x) * frames):
        c_ref[img, 0] = jnp.zeros((32, 128), jnp.float32)
        c_ref[img, row_blocks + 1] = jnp.zeros((32, 128), jnp.float32)

        def column_sums(a, carry):
            c_ref[img, a, 0:8, :] += moved(c_ref[img, a, 8:16, :])
            c_ref[img, a, 16:24, :] += moved(c_ref[img, a, 24:32, :])
            return carry

        lax.fori_loop(1, row_blocks + 1, column_sums, 0, unroll=4)

        def row_sums(k, carry):
            blocks = []
            for half in range(2):
                a = 2 * k + half + 1
                value = c_ref[img, a, 0:8, :]
                value += jnp.where(sub % 4 == 0, c_ref[img, a - 1, 16:24, :], 0.0)
                value += jnp.where(sub % 4 == 3, c_ref[img, a + 1, 16:24, :], 0.0)
                blocks.append(value)
            start = pl.multiple_of(k * 8, 8)
            d_ref[img, pl.ds(start, 8), 0:128] = jnp.where(sub < 4, blocks[0], pltpu.roll(blocks[1], 4, 0))
            d_ref[img, pl.ds(start, 8), 128:256] = jnp.where(sub < 4, pltpu.roll(blocks[0], 4, 0), blocks[1])
            return carry

        lax.fori_loop(0, rows // 8, row_sums, 0, unroll=4)
        emit(img // frames, img % frames, mm(d_ref[img].astype(kind), gather))


def scratch(pairs, frames, rows):
    images = pairs * frames
    return [
        pltpu.VMEM((pairs * 2, rows + 16, 512), jnp.float32),
        pltpu.VMEM((images, rows // 4 + 2, 160, 256), jnp.bfloat16),
        pltpu.VMEM((images, rows // 4 + 2, 32, 128), jnp.float32),
        pltpu.VMEM((images, rows, 256), jnp.float32),
    ]


def z_kernel(measured, states, response, own, other, cosine, sines, w_first, b_first, w_mid, b_mid, w_last, spread, gather, data_out, res_out, *scratches):
    kind = jnp.bfloat16
    cos, sin = cosine[...], sines[...]
    source = (measured[...] + states[0]).astype(kind)
    row_real = mm(source, cos).astype(kind)
    row_imag = (-mm(source, sin)).astype(kind)
    gain = 1.0 / (1.0 + response[...])
    spec_real = ((mm(cos, row_real) + mm(sin, row_imag)) * gain).astype(kind)
    spec_imag = ((mm(cos, row_imag) - mm(sin, row_real)) * gain).astype(kind)
    back_real = (mm(cos, spec_real) - mm(sin, spec_imag)).astype(kind)
    back_imag = (mm(cos, spec_imag) + mm(sin, spec_real)).astype(kind)
    data_out[...] = (mm(back_real, cos) - mm(back_imag, sin)) * (1.0 / (source.shape[0] * source.shape[1]))

    def emit(pair, f, value):
        res_out[...] = value.astype(kind)

    denoise([(lambda: own[...], lambda: other[...])], w_first.at[0], b_first.at[0], w_mid.at[0], b_mid.at[0], w_last.at[0], spread[...], gather[...], emit, *scratches, frames=1)


def xy_kernel(planes, w_first, b_first, w_mid, b_mid, w_last, spread, gather, res_out, *scratches):
    for which in range(2):

        def emit(pair, f, value):
            res_out[which, pair, f] = value.astype(jnp.bfloat16)

        pairs = [(lambda p=p: planes[which, p, 0], lambda p=p: planes[which, p, 1]) for p in range(2)]
        d = which + 1
        denoise(pairs, w_first.at[d], b_first.at[d], w_mid.at[d], b_mid.at[d], w_last.at[d], spread[...], gather[...], emit, *scratches, frames=2)


def final_kernel(states, data, res_z, back_x, back_y, out):
    w = [states[k] for k in range(4)]
    res_x = jnp.transpose(back_x[...].astype(jnp.float32))
    z = [
        2.0 * data[...] - w[0],
        w[1] - 2.0 * res_z[...].astype(jnp.float32),
        w[2] - 2.0 * res_x,
        w[3] - 2.0 * back_y[...].astype(jnp.float32),
    ]
    twice = 0.5 * (z[0] + z[1] + z[2] + z[3])
    for k in range(4):
        out[k] = (1.0 - relaxation) * w[k] + relaxation * (twice - z[k])


VM = pl.BlockSpec(memory_space=pltpu.VMEM)


def call(kernel, out_shape, args, scratch_shapes, flops):
    return pl.pallas_call(
        kernel,
        out_shape=out_shape,
        in_specs=[VM] * len(args),
        out_specs=jax.tree.map(lambda _: VM, out_shape),
        scratch_shapes=scratch_shapes,
        compiler_params=pltpu.CompilerParams(vmem_limit_bytes=56 * 2**20),
        cost_estimate=pl.CostEstimate(flops=flops, bytes_accessed=2**21, transcendentals=0),
    )(*args)


def fourier_tables(length):
    indices = jnp.arange(length, dtype=jnp.int32)
    phase = indices[:, None] * indices[None, :] % length
    angle = phase.astype(jnp.float32) * (2.0 * math.pi / length)
    return (jnp.cos(angle).astype(jnp.bfloat16), jnp.sin(angle).astype(jnp.bfloat16))


def on_device(states, measured, response, kernel_in, bias_in, kernel_mid, bias_mid, kernel_out):
    kind = jnp.bfloat16
    current = states[:, 0, 0]
    width = current.shape[-1]
    rounded = current[1:].astype(kind)
    devices = lax.axis_size("frame") * lax.axis_size("plane")
    depth = lax.axis_size("plane")
    partner = lax.ppermute(rounded[0], "frame", [(0, 1), (1, 0)])
    leaving = jnp.stack([jnp.transpose(rounded[1]), rounded[2]])
    leaving = leaving.reshape(2, devices, width // devices, width).transpose(1, 0, 2, 3)
    arrived = lax.all_to_all(leaving, ("frame", "plane"), split_axis=0, concat_axis=0, tiled=True)
    planes = arrived.reshape(2, depth, 2, width // devices, width).transpose(2, 3, 0, 1, 4)
    weights = banded(kernel_in, bias_in, kernel_mid, bias_mid, kernel_out)
    cosine, sines = fourier_tables(width)
    spread = jnp.asarray(spread_table(width), kind)
    gather = jnp.asarray(gather_table(width), kind)
    image = jax.ShapeDtypeStruct((width, width), kind)
    data, res_z = call(
        z_kernel,
        (jax.ShapeDtypeStruct((width, width), jnp.float32), image),
        (measured[0, 0], current, response, rounded[0], partner, cosine, sines) + weights + (spread, gather),
        scratch(1, 1, width),
        4 * 10**9,
    )
    residuals = call(
        xy_kernel,
        jax.ShapeDtypeStruct((2, 2, 2, depth, width), kind),
        (planes,) + weights + (spread, gather),
        scratch(2, 2, depth),
        8 * 10**9,
    )
    returning = residuals.transpose(2, 3, 0, 1, 4).reshape(devices, 2, width // devices, width)
    returned = lax.all_to_all(returning, ("frame", "plane"), split_axis=0, concat_axis=0, tiled=True)
    returned = returned.transpose(1, 0, 2, 3).reshape(2, width, width)
    out = call(
        final_kernel,
        jax.ShapeDtypeStruct(current.shape, jnp.float32),
        (current, data, res_z, returned[0], returned[1]),
        [],
        10**6,
    )
    return out[:, None, None]


def solution(mesh):
    placed = (
        P(None, "frame", "plane", None, None),
        P("frame", "plane", None, None),
        P(),
        P(),
        P(),
        P(),
        P(),
        P(),
    )
    return jax.shard_map(
        on_device,
        mesh=mesh,
        in_specs=placed,
        out_specs=P(None, "frame", "plane", None, None),
        check_vma=False,
    )
```

```python
import functools
import math

import jax
import jax.numpy as jnp
import numpy as np
from jax import lax
from jax.experimental import pallas as pl
from jax.experimental.pallas import tpu as pltpu
from jax.sharding import PartitionSpec as P

relaxation = 0.8

GROUPS = [(0, 0), (0, 1), (3, 0), (3, 1), (1, 0), (1, 1), (2, 0), (2, 1)]
STRIP = 16
FIRST_STEP = 8
MID_STEP = 16


def block_order(width):
    blocks = width // 2
    per = blocks // STRIP
    lane = np.arange(blocks)
    return (lane % STRIP) * per + lane // STRIP


def spread_table(width):
    blocks = width // 2
    order = block_order(width)
    table = np.zeros((width, 4 * blocks), np.float32)
    for xo in range(4):
        for lane in range(blocks):
            col = 2 * order[lane] + xo - 1
            if 0 <= col < width:
                table[col, xo * blocks + lane] = 1
    return table


def gather_table(width):
    blocks = width // 2
    order = block_order(width)
    table = np.zeros((width, width), np.float32)
    for j in range(2):
        for lane in range(blocks):
            table[j * blocks + lane, 2 * order[lane] + j] = 1
    return table


def select_in():
    chosen = np.zeros((9, 4, 24, 2, 8), np.float32)
    for half in range(2):
        for g, (i, j) in enumerate(GROUPS):
            for p in range(3):
                for q in range(3):
                    chosen[3 * p + q, j + q, 7 + 4 * half + i + p, half, g] = 1
    return chosen.reshape(9, 96, 16)


def slots_mid():
    slots = list(GROUPS)
    slots += [(i, -1 if j == 1 else 2) for i, j in GROUPS]
    slots += [(-1 if i == 3 else 4, j) for i, j in GROUPS[:4]]
    slots += [(-1 if i == 3 else 4, -1 if j == 1 else 2) for i, j in GROUPS[:4]]
    return slots


def select_mid():
    chosen = np.zeros((9, 24, 8), np.float32)
    for s, (row, col) in enumerate(slots_mid()):
        for g, (i, j) in enumerate(GROUPS):
            p, q = row - i + 1, col - j + 1
            if 0 <= p < 3 and 0 <= q < 3:
                chosen[3 * p + q, s, g] = 1
    return chosen


def select_out():
    targets = [None] * 32
    for j in range(2):
        far = 2 if j == 0 else -1
        for i in range(4):
            targets[j * 4 + i] = (i, j)
            targets[8 + j * 4 + i] = (i, far)
        for base, col in ((16, j), (24, far)):
            targets[base + j * 4] = (4, col)
            targets[base + j * 4 + 3] = (-1, col)
    chosen = np.zeros((9, 32, 8), np.float32)
    for r, target in enumerate(targets):
        if target is None:
            continue
        for g, (i, j) in enumerate(GROUPS):
            p, q = i - target[0] + 1, j - target[1] + 1
            if 0 <= p < 3 and 0 <= q < 3:
                chosen[3 * p + q, r, g] = 1
    return chosen


def first_table():
    chosen = select_in()
    table = np.zeros((2, 96, 16, 32), np.float32)
    for ch in range(2):
        for tap in range(9):
            table[ch, :, :, 2 * tap + ch] = chosen[tap]
    return table.reshape(192, 512)


def last_table():
    table = np.zeros((32, 8, 16), np.float32)
    table[:, :, :9] = select_out().transpose(1, 2, 0)
    return table.reshape(32, 128)


def mm(a, b, dims=((1,), (0,))):
    return lax.dot_general(a, b, (dims, ((), ())), preferred_element_type=jnp.float32)


def prepare(d, params, tables, built, frames):
    kernel_in, bias_in, kernel_mid, bias_mid, kernel_out = params
    first_at, last_at = tables
    w_first, b_first, w_mid, b_mid, w_last, spare = built
    kind = jnp.bfloat16
    lane = lax.broadcasted_iota(jnp.int32, (32, 512), 1)
    row = lax.broadcasted_iota(jnp.int32, (32, 512), 0)
    repeat = (lane % 32 == row).astype(jnp.float32)
    wide = repeat.astype(kind)
    narrow = wide[:, :256]

    spare[...] = jnp.zeros_like(spare)
    for tap in range(9):
        spare[2 * tap:2 * tap + 2, :] = mm(kernel_in[d, tap], wide, ((0,), (0,)))
    tiled = jnp.concatenate([spare[...]] * 16, 0)
    own = lax.broadcasted_iota(jnp.int32, (512, 512), 0) // 32 == lax.broadcasted_iota(jnp.int32, (512, 512), 1) // 32
    built_first = mm(first_at[...], jnp.where(own, tiled, 0.0).astype(kind)).astype(kind)
    w_first[:, 0:512] = built_first
    exact = lax.dot_general(bias_in[...], repeat, (((1,), (0,)), ((), ())), precision=lax.Precision.HIGHEST, preferred_element_type=jnp.float32)
    b_first[0:1, 0:512] = exact[d:d + 1]
    if frames == 2:
        w_first[0:96, 512:1024] = built_first[96:192]
        w_first[96:192, 512:1024] = built_first[0:96]
        b_first[0:1, 512:1024] = exact[d:d + 1]
    exact = lax.dot_general(bias_mid[:, 0, :], repeat[:, :256], (((1,), (0,)), ((), ())), precision=lax.Precision.HIGHEST, preferred_element_type=jnp.float32)
    b_mid[0:1, :] = exact[d:d + 1]

    taps = [mm(kernel_mid[d, 0, tap], narrow, ((0,), (0,))) for tap in range(9)]
    group = lane[:, :256] // 32
    for s, (r, c) in enumerate(slots_mid()):
        value = jnp.zeros((32, 256), jnp.float32)
        for g, (i, j) in enumerate(GROUPS):
            p, q = r - i + 1, c - j + 1
            if 0 <= p < 3 and 0 <= q < 3:
                value = jnp.where(group == g, taps[3 * p + q], value)
        w_mid[s * 32:(s + 1) * 32, :] = value.astype(kind)

    spare[9:16, 0:256] = jnp.zeros((7, 256), jnp.float32)
    spare[0:9, 0:256] = mm(kernel_out[d], narrow)
    tiled = jnp.concatenate([spare[0:16, 0:256]] * 8, 0)
    own = lax.broadcasted_iota(jnp.int32, (128, 256), 0) // 16 == lax.broadcasted_iota(jnp.int32, (128, 256), 1) // 32
    w_last[...] = mm(last_at[...], jnp.where(own, tiled, 0.0).astype(kind)).astype(kind)


def denoise(x, built, spread, gather, emit, u_ref, h_ref, c_ref, frames):
    w_first, b_first, w_mid, b_mid, w_last, _ = built
    rows = u_ref.shape[1] - 16
    row_blocks = rows // 4
    images = len(x) * frames
    kind = jnp.bfloat16
    for pair in range(len(x)):
        for ch in range(2):
            u_ref[pair * 2 + ch, :8, :] = jnp.zeros((8, 512), jnp.float32)
            u_ref[pair * 2 + ch, rows + 8:, :] = jnp.zeros((8, 512), jnp.float32)
            u_ref[pair * 2 + ch, 8:rows + 8, :] = mm(x[pair][ch](), spread)
    for img in range(images):
        h_ref[img, 0] = jnp.zeros((160, 256), kind)
        h_ref[img, row_blocks + 1] = jnp.zeros((160, 256), kind)
        c_ref[img, 0] = jnp.zeros((32, 128), jnp.float32)
        c_ref[img, row_blocks + 1] = jnp.zeros((32, 128), jnp.float32)

    strip = lax.broadcasted_iota(jnp.int32, (16, 256), 0)
    first_strip = strip == 0
    last_strip = strip == 15

    def first_layer(step, carry):
        for pair in range(len(x)):
            parts = []
            for ch in range(2):
                for xo in range(4):
                    parts.append(jnp.concatenate([
                        u_ref[pair * 2 + ch, pl.ds(pl.multiple_of((step * FIRST_STEP + k) * 8, 8), 24), xo * 128:(xo + 1) * 128]
                        for k in range(FIRST_STEP)], 1))
            stacked = jnp.concatenate(parts, 0).astype(kind)
            made = mm(stacked, w_first[...], ((0,), (0,)))
            made = jnp.maximum(made + b_first[0:1, :], 0.0)
            for f in range(frames):
                for k in range(FIRST_STEP):
                    for half in range(2):
                        at = f * 512 + half * 256
                        piece = made[k * 128:(k + 1) * 128, at:at + 256]
                        to = h_ref.at[pair * frames + f, 2 * (step * FIRST_STEP + k) + half + 1]
                        to[16:144, :] = piece.astype(kind)
                        to[0:16, :] = jnp.where(first_strip, 0.0, pltpu.roll(piece[112:128], 1, 0)).astype(kind)
                        to[144:160, :] = jnp.where(last_strip, 0.0, pltpu.roll(piece[0:16], 15, 0)).astype(kind)
        return carry

    lax.fori_loop(0, rows // 8 // FIRST_STEP, first_layer, 0)

    n = MID_STEP * 128
    right = (lax.broadcasted_iota(jnp.int32, (n, 256), 1) // 32) % 2 == 1
    right_half = right[:, :128]
    low = lax.broadcasted_iota(jnp.int32, (n, 128), 1) >= 64
    steps = row_blocks // MID_STEP

    def mid_layer(at, carry):
        img, a = at // steps, (at % steps) * MID_STEP

        def part(down, shift, lanes):
            return h_ref[img, pl.ds(a + 1 + down, MID_STEP), 16 + shift:144 + shift, 0:lanes].reshape(n, lanes)

        here = part(0, 0, 256)
        side = jnp.where(right, part(0, -16, 256), part(0, 16, 256))
        across = jnp.where(low, part(-1, 0, 128), part(1, 0, 128))
        corner_left = jnp.where(low, part(-1, -16, 128), part(1, -16, 128))
        corner_right = jnp.where(low, part(-1, 16, 128), part(1, 16, 128))
        corner = jnp.where(right_half, corner_left, corner_right)
        made = mm(jnp.concatenate([here, side, across, corner], 1), w_mid[...])
        hidden = jnp.maximum(made + b_mid[0:1, :], 0.0).astype(kind)
        last = mm(w_last[...], hidden, ((1,), (1,)))
        for k in range(MID_STEP):
            c_ref[img, a + 1 + k] = last[:, k * 128:(k + 1) * 128]
        return carry

    lax.fori_loop(0, images * steps, mid_layer, 0)

    lane = lax.broadcasted_iota(jnp.int32, (row_blocks * 8, 128), 1)
    sub = lax.broadcasted_iota(jnp.int32, (row_blocks * 8, 128), 0) % 8
    half_sub = sub[:row_blocks * 4]

    def moved(value):
        before = jnp.where(lane >= 16, pltpu.roll(value, 16, 1), jnp.where(lane >= 1, pltpu.roll(value, 17, 1), 0.0))
        after = jnp.where(lane < 112, pltpu.roll(value, 112, 1), jnp.where(lane < 127, pltpu.roll(value, 111, 1), 0.0))
        return jnp.where(sub < 4, before, after)

    for img in range(images):

        def piece(at, down=0):
            return c_ref[img, 1 + down:1 + down + row_blocks, at:at + 8, :].reshape(row_blocks * 8, 128)

        total = piece(0) + moved(piece(8))
        edges = piece(16) + moved(piece(24))
        c_ref[img, 1:1 + row_blocks, 16:24, :] = edges.reshape(row_blocks, 8, 128)
        total += jnp.where(sub % 4 == 0, piece(16, -1), 0.0) + jnp.where(sub % 4 == 3, piece(16, 1), 0.0)
        twos = total.reshape(row_blocks // 2, 16, 128)
        even = twos[:, 0:8].reshape(row_blocks * 4, 128)
        odd = twos[:, 8:16].reshape(row_blocks * 4, 128)
        left = jnp.where(half_sub < 4, even, pltpu.roll(odd, 4, 0))
        right_side = jnp.where(half_sub < 4, pltpu.roll(even, rows - 4, 0), odd)
        emit(img // frames, img % frames, mm(jnp.concatenate([left, right_side], 1).astype(kind), gather))


def scratch(pairs, frames, rows):
    images = pairs * frames
    return [
        pltpu.VMEM((192, frames * 512), jnp.bfloat16),
        pltpu.VMEM((8, frames * 512), jnp.float32),
        pltpu.VMEM((768, 256), jnp.bfloat16),
        pltpu.VMEM((8, 256), jnp.float32),
        pltpu.VMEM((32, 256), jnp.bfloat16),
        pltpu.VMEM((32, 512), jnp.float32),
        pltpu.VMEM((pairs * 2, rows + 16, 512), jnp.float32),
        pltpu.VMEM((images, rows // 4 + 2, 160, 256), jnp.bfloat16),
        pltpu.VMEM((images, rows // 4 + 2, 32, 128), jnp.float32),
    ]


def z_kernel(measured, states, response, own, other, cosine, sines, *rest):
    params, tables, spread, gather, data_out, res_out = rest[:5], rest[5:7], rest[7], rest[8], rest[9], rest[10]
    built, work = rest[11:17], rest[17:]
    kind = jnp.bfloat16
    cos, sin = cosine[...], sines[...]
    source = (measured[...] + states[0]).astype(kind)
    row_real = mm(source, cos).astype(kind)
    row_imag = (-mm(source, sin)).astype(kind)
    gain = 1.0 / (1.0 + response[...])
    spec_real = ((mm(cos, row_real) + mm(sin, row_imag)) * gain).astype(kind)
    spec_imag = ((mm(cos, row_imag) - mm(sin, row_real)) * gain).astype(kind)
    back_real = (mm(cos, spec_real) - mm(sin, spec_imag)).astype(kind)
    back_imag = (mm(cos, spec_imag) + mm(sin, spec_real)).astype(kind)
    data_out[...] = (mm(back_real, cos) - mm(back_imag, sin)) * (1.0 / (source.shape[0] * source.shape[1]))

    def emit(pair, f, value):
        res_out[...] = value.astype(kind)

    prepare(0, params, tables, built, 1)
    denoise([(lambda: own[...], lambda: other[...])], built, spread[...], gather[...], emit, *work, frames=1)


def xy_kernel(planes, *rest):
    params, tables, spread, gather, res_out = rest[:5], rest[5:7], rest[7], rest[8], rest[9]
    built, work = rest[10:16], rest[16:]
    for which in range(2):

        def emit(pair, f, value):
            res_out[which, pair, f] = value.astype(jnp.bfloat16)

        pairs = [(lambda p=p: planes[which, p, 0], lambda p=p: planes[which, p, 1]) for p in range(2)]
        prepare(which + 1, params, tables, built, 2)
        denoise(pairs, built, spread[...], gather[...], emit, *work, frames=2)


def final_kernel(states, data, res_z, back_x, back_y, out):
    w = [states[k] for k in range(4)]
    res_x = jnp.transpose(back_x[...].astype(jnp.float32))
    z = [
        2.0 * data[...] - w[0],
        w[1] - 2.0 * res_z[...].astype(jnp.float32),
        w[2] - 2.0 * res_x,
        w[3] - 2.0 * back_y[...].astype(jnp.float32),
    ]
    twice = 0.5 * (z[0] + z[1] + z[2] + z[3])
    for k in range(4):
        out[k] = (1.0 - relaxation) * w[k] + relaxation * (twice - z[k])


VM = pl.BlockSpec(memory_space=pltpu.VMEM)


def call(kernel, out_shape, args, scratch_shapes, flops):
    return pl.pallas_call(
        kernel,
        out_shape=out_shape,
        in_specs=[VM] * len(args),
        out_specs=jax.tree.map(lambda _: VM, out_shape),
        scratch_shapes=scratch_shapes,
        compiler_params=pltpu.CompilerParams(vmem_limit_bytes=56 * 2**20),
        cost_estimate=pl.CostEstimate(flops=flops, bytes_accessed=2**21, transcendentals=0),
    )(*args)


def fourier_tables(length):
    indices = np.arange(length, dtype=np.int32)
    phase = indices[:, None] * indices[None, :] % length
    angle = phase.astype(np.float32) * np.float32(2.0 * math.pi / length)
    return (jnp.asarray(np.cos(angle), jnp.bfloat16), jnp.asarray(np.sin(angle), jnp.bfloat16))


def constants(width):
    kind = jnp.bfloat16
    tables = (first_table(), last_table(), spread_table(width), gather_table(width))
    return tuple(jnp.asarray(table.astype(kind)) for table in tables)


def on_device(states, measured, response, kernel_in, bias_in, kernel_mid, bias_mid, kernel_out):
    kind = jnp.bfloat16
    current = states[:, 0, 0]
    width = current.shape[-1]
    rounded = current[1:].astype(kind)
    devices = lax.axis_size("frame") * lax.axis_size("plane")
    depth = lax.axis_size("plane")
    partner = lax.ppermute(rounded[0], "frame", [(0, 1), (1, 0)])
    leaving = jnp.stack([jnp.transpose(rounded[1]), rounded[2]])
    leaving = leaving.reshape(2, devices, width // devices, width).transpose(1, 0, 2, 3)
    arrived = lax.all_to_all(leaving, ("frame", "plane"), split_axis=0, concat_axis=0, tiled=True)
    planes = arrived.reshape(2, depth, 2, width // devices, width).transpose(2, 3, 0, 1, 4)
    weights = (kernel_in, bias_in, kernel_mid, bias_mid, kernel_out)
    cosine, sines = fourier_tables(width)
    tables = constants(width)
    image = jax.ShapeDtypeStruct((width, width), kind)
    data, res_z = call(
        z_kernel,
        (jax.ShapeDtypeStruct((width, width), jnp.float32), image),
        (measured[0, 0], current, response, rounded[0], partner, cosine, sines) + weights + tables,
        scratch(1, 1, width),
        4 * 10**9,
    )
    residuals = call(
        xy_kernel,
        jax.ShapeDtypeStruct((2, 2, 2, depth, width), kind),
        (planes,) + weights + tables,
        scratch(2, 2, depth),
        8 * 10**9,
    )
    returning = residuals.transpose(2, 3, 0, 1, 4).reshape(devices, 2, width // devices, width)
    returned = lax.all_to_all(returning, ("frame", "plane"), split_axis=0, concat_axis=0, tiled=True)
    returned = returned.transpose(1, 0, 2, 3).reshape(2, width, width)
    out = call(
        final_kernel,
        jax.ShapeDtypeStruct(current.shape, jnp.float32),
        (current, data, res_z, returned[0], returned[1]),
        [],
        10**6,
    )
    return out[:, None, None]


def solution(mesh):
    placed = (
        P(None, "frame", "plane", None, None),
        P("frame", "plane", None, None),
        P(),
        P(),
        P(),
        P(),
        P(),
        P(),
    )
    return jax.shard_map(
        on_device,
        mesh=mesh,
        in_specs=placed,
        out_specs=P(None, "frame", "plane", None, None),
        check_vma=False,
    )
```

```python
import functools
import math

import jax
import jax.numpy as jnp
import numpy as np
from jax import lax
from jax.experimental import pallas as pl
from jax.experimental.pallas import tpu as pltpu
from jax.sharding import PartitionSpec as P

relaxation = 0.8
MESH = pl.DeviceIdType.MESH
UNROLL = 8

GROUPS = [(0, 0), (0, 1), (3, 0), (3, 1), (1, 0), (1, 1), (2, 0), (2, 1)]
STRIP = 16
FIRST_STEP = 8
MID_STEP = 16


def block_order(width):
    blocks = width // 2
    per = blocks // STRIP
    lane = np.arange(blocks)
    return (lane % STRIP) * per + lane // STRIP


def spread_table(width):
    blocks = width // 2
    order = block_order(width)
    table = np.zeros((width, 4 * blocks), np.float32)
    for xo in range(4):
        for lane in range(blocks):
            col = 2 * order[lane] + xo - 1
            if 0 <= col < width:
                table[col, xo * blocks + lane] = 1
    return table


def gather_table(width):
    blocks = width // 2
    order = block_order(width)
    table = np.zeros((width, width), np.float32)
    for j in range(2):
        for lane in range(blocks):
            table[j * blocks + lane, 2 * order[lane] + j] = 1
    return table


def select_in():
    chosen = np.zeros((9, 4, 24, 2, 8), np.float32)
    for half in range(2):
        for g, (i, j) in enumerate(GROUPS):
            for p in range(3):
                for q in range(3):
                    chosen[3 * p + q, j + q, 7 + 4 * half + i + p, half, g] = 1
    return chosen.reshape(9, 96, 16)


def slots_mid():
    slots = list(GROUPS)
    slots += [(i, -1 if j == 1 else 2) for i, j in GROUPS]
    slots += [(-1 if i == 3 else 4, j) for i, j in GROUPS[:4]]
    slots += [(-1 if i == 3 else 4, -1 if j == 1 else 2) for i, j in GROUPS[:4]]
    return slots


def select_mid():
    chosen = np.zeros((9, 24, 8), np.float32)
    for s, (row, col) in enumerate(slots_mid()):
        for g, (i, j) in enumerate(GROUPS):
            p, q = row - i + 1, col - j + 1
            if 0 <= p < 3 and 0 <= q < 3:
                chosen[3 * p + q, s, g] = 1
    return chosen


def select_out():
    targets = [None] * 32
    for j in range(2):
        far = 2 if j == 0 else -1
        for i in range(4):
            targets[j * 4 + i] = (i, j)
            targets[8 + j * 4 + i] = (i, far)
        for base, col in ((16, j), (24, far)):
            targets[base + j * 4] = (4, col)
            targets[base + j * 4 + 3] = (-1, col)
    chosen = np.zeros((9, 32, 8), np.float32)
    for r, target in enumerate(targets):
        if target is None:
            continue
        for g, (i, j) in enumerate(GROUPS):
            p, q = i - target[0] + 1, j - target[1] + 1
            if 0 <= p < 3 and 0 <= q < 3:
                chosen[3 * p + q, r, g] = 1
    return chosen


def first_table():
    chosen = select_in()
    table = np.zeros((2, 96, 16, 32), np.float32)
    for ch in range(2):
        for tap in range(9):
            table[ch, :, :, 2 * tap + ch] = chosen[tap]
    return table.reshape(192, 512)


def last_table():
    table = np.zeros((32, 8, 16), np.float32)
    table[:, :, :9] = select_out().transpose(1, 2, 0)
    return table.reshape(32, 128)


def mm(a, b, dims=((1,), (0,))):
    return lax.dot_general(a, b, (dims, ((), ())), preferred_element_type=jnp.float32)


def prepare(d, params, tables, built, frames):
    kernel_in, bias_in, kernel_mid, bias_mid, kernel_out = params
    first_at, last_at = tables
    w_first, b_first, w_mid, b_mid, w_last, spare = built
    kind = jnp.bfloat16
    lane = lax.broadcasted_iota(jnp.int32, (32, 512), 1)
    row = lax.broadcasted_iota(jnp.int32, (32, 512), 0)
    repeat = (lane % 32 == row).astype(jnp.float32)
    wide = repeat.astype(kind)
    narrow = wide[:, :256]

    spare[...] = jnp.zeros_like(spare)
    for tap in range(9):
        spare[2 * tap:2 * tap + 2, :] = mm(kernel_in[d, tap], wide, ((0,), (0,)))
    tiled = jnp.concatenate([spare[...]] * 16, 0)
    own = lax.broadcasted_iota(jnp.int32, (512, 512), 0) // 32 == lax.broadcasted_iota(jnp.int32, (512, 512), 1) // 32
    built_first = mm(first_at[...], jnp.where(own, tiled, 0.0).astype(kind)).astype(kind)
    w_first[:, 0:512] = built_first
    exact = lax.dot_general(bias_in[...], repeat, (((1,), (0,)), ((), ())), precision=lax.Precision.HIGHEST, preferred_element_type=jnp.float32)
    b_first[0:1, 0:512] = exact[d:d + 1]
    if frames == 2:
        w_first[0:96, 512:1024] = built_first[96:192]
        w_first[96:192, 512:1024] = built_first[0:96]
        b_first[0:1, 512:1024] = exact[d:d + 1]
    exact = lax.dot_general(bias_mid[:, 0, :], repeat[:, :256], (((1,), (0,)), ((), ())), precision=lax.Precision.HIGHEST, preferred_element_type=jnp.float32)
    b_mid[0:1, :] = exact[d:d + 1]

    taps = [mm(kernel_mid[d, 0, tap], narrow, ((0,), (0,))) for tap in range(9)]
    group = lane[:, :256] // 32
    for s, (r, c) in enumerate(slots_mid()):
        value = jnp.zeros((32, 256), jnp.float32)
        for g, (i, j) in enumerate(GROUPS):
            p, q = r - i + 1, c - j + 1
            if 0 <= p < 3 and 0 <= q < 3:
                value = jnp.where(group == g, taps[3 * p + q], value)
        w_mid[s * 32:(s + 1) * 32, :] = value.astype(kind)

    spare[9:16, 0:256] = jnp.zeros((7, 256), jnp.float32)
    spare[0:9, 0:256] = mm(kernel_out[d], narrow)
    tiled = jnp.concatenate([spare[0:16, 0:256]] * 8, 0)
    own = lax.broadcasted_iota(jnp.int32, (128, 256), 0) // 16 == lax.broadcasted_iota(jnp.int32, (128, 256), 1) // 32
    w_last[...] = mm(last_at[...], jnp.where(own, tiled, 0.0).astype(kind)).astype(kind)


def first_half(x, built, spread, u_ref, h_ref, c_ref, frames):
    w_first, b_first = built[:2]
    rows = u_ref.shape[1] - 16
    row_blocks = rows // 4
    images = len(x) * frames
    kind = jnp.bfloat16
    for pair in range(len(x)):
        for ch in range(2):
            u_ref[pair * 2 + ch, :8, :] = jnp.zeros((8, 512), jnp.float32)
            u_ref[pair * 2 + ch, rows + 8:, :] = jnp.zeros((8, 512), jnp.float32)
            u_ref[pair * 2 + ch, 8:rows + 8, :] = mm(x[pair][ch](), spread)
    for img in range(images):
        h_ref[img, 0] = jnp.zeros((160, 256), kind)
        h_ref[img, row_blocks + 1] = jnp.zeros((160, 256), kind)
        c_ref[img, 0] = jnp.zeros((32, 128), jnp.float32)
        c_ref[img, row_blocks + 1] = jnp.zeros((32, 128), jnp.float32)

    strip = lax.broadcasted_iota(jnp.int32, (16, 256), 0)
    first_strip = strip == 0
    last_strip = strip == 15

    def first_layer(step, carry):
        for pair in range(len(x)):
            parts = []
            for ch in range(2):
                for xo in range(4):
                    parts.append(jnp.concatenate([
                        u_ref[pair * 2 + ch, pl.ds(pl.multiple_of((step * FIRST_STEP + k) * 8, 8), 24), xo * 128:(xo + 1) * 128]
                        for k in range(FIRST_STEP)], 1))
            stacked = jnp.concatenate(parts, 0).astype(kind)
            made = mm(stacked, w_first[...], ((0,), (0,)))
            made = jnp.maximum(made + b_first[0:1, :], 0.0)
            for f in range(frames):
                for k in range(FIRST_STEP):
                    for half in range(2):
                        at = f * 512 + half * 256
                        piece = made[k * 128:(k + 1) * 128, at:at + 256]
                        to = h_ref.at[pair * frames + f, 2 * (step * FIRST_STEP + k) + half + 1]
                        to[16:144, :] = piece.astype(kind)
                        to[0:16, :] = jnp.where(first_strip, 0.0, pltpu.roll(piece[112:128], 1, 0)).astype(kind)
                        to[144:160, :] = jnp.where(last_strip, 0.0, pltpu.roll(piece[0:16], 15, 0)).astype(kind)
        return carry

    lax.fori_loop(0, rows // 8 // FIRST_STEP, first_layer, 0)


def second_half(built, gather, emit, h_ref, c_ref, frames):
    w_mid, b_mid, w_last = built[2:5]
    images = h_ref.shape[0]
    row_blocks = h_ref.shape[1] - 2
    rows = row_blocks * 4
    kind = jnp.bfloat16
    n = MID_STEP * 128
    right = (lax.broadcasted_iota(jnp.int32, (n, 256), 1) // 32) % 2 == 1
    right_half = right[:, :128]
    low = lax.broadcasted_iota(jnp.int32, (n, 128), 1) >= 64
    steps = row_blocks // MID_STEP

    def mid_layer(at, carry):
        img, a = at // steps, (at % steps) * MID_STEP

        def part(down, shift, lanes):
            return h_ref[img, pl.ds(a + 1 + down, MID_STEP), 16 + shift:144 + shift, 0:lanes].reshape(n, lanes)

        here = part(0, 0, 256)
        side = jnp.where(right, part(0, -16, 256), part(0, 16, 256))
        across = jnp.where(low, part(-1, 0, 128), part(1, 0, 128))
        corner_left = jnp.where(low, part(-1, -16, 128), part(1, -16, 128))
        corner_right = jnp.where(low, part(-1, 16, 128), part(1, 16, 128))
        corner = jnp.where(right_half, corner_left, corner_right)
        made = mm(jnp.concatenate([here, side, across, corner], 1), w_mid[...])
        hidden = jnp.maximum(made + b_mid[0:1, :], 0.0).astype(kind)
        last = mm(w_last[...], hidden, ((1,), (1,)))
        for k in range(MID_STEP):
            c_ref[img, a + 1 + k] = last[:, k * 128:(k + 1) * 128]
        return carry

    lax.fori_loop(0, images * steps, mid_layer, 0)

    lane = lax.broadcasted_iota(jnp.int32, (row_blocks * 8, 128), 1)
    sub = lax.broadcasted_iota(jnp.int32, (row_blocks * 8, 128), 0) % 8
    half_sub = sub[:row_blocks * 4]

    def moved(value):
        before = jnp.where(lane >= 16, pltpu.roll(value, 16, 1), jnp.where(lane >= 1, pltpu.roll(value, 17, 1), 0.0))
        after = jnp.where(lane < 112, pltpu.roll(value, 112, 1), jnp.where(lane < 127, pltpu.roll(value, 111, 1), 0.0))
        return jnp.where(sub < 4, before, after)

    for img in range(images):

        def piece(at, down=0):
            return c_ref[img, 1 + down:1 + down + row_blocks, at:at + 8, :].reshape(row_blocks * 8, 128)

        total = piece(0) + moved(piece(8))
        edges = piece(16) + moved(piece(24))
        c_ref[img, 1:1 + row_blocks, 16:24, :] = edges.reshape(row_blocks, 8, 128)
        total += jnp.where(sub % 4 == 0, piece(16, -1), 0.0) + jnp.where(sub % 4 == 3, piece(16, 1), 0.0)
        twos = total.reshape(row_blocks // 2, 16, 128)
        even = twos[:, 0:8].reshape(row_blocks * 4, 128)
        odd = twos[:, 8:16].reshape(row_blocks * 4, 128)
        left = jnp.where(half_sub < 4, even, pltpu.roll(odd, 4, 0))
        right_side = jnp.where(half_sub < 4, pltpu.roll(even, rows - 4, 0), odd)
        emit(img // frames, img % frames, mm(jnp.concatenate([left, right_side], 1).astype(kind), gather))


def built_shapes(frames):
    return [
        pltpu.VMEM((192, frames * 512), jnp.bfloat16),
        pltpu.VMEM((8, frames * 512), jnp.float32),
        pltpu.VMEM((768, 256), jnp.bfloat16),
        pltpu.VMEM((8, 256), jnp.float32),
        pltpu.VMEM((32, 256), jnp.bfloat16),
        pltpu.VMEM((32, 512), jnp.float32),
    ]


def work_shapes(pairs, frames, rows):
    images = pairs * frames
    return [
        pltpu.VMEM((pairs * 2, rows + 16, 512), jnp.float32),
        pltpu.VMEM((images, rows // 4 + 2, 160, 256), jnp.bfloat16),
        pltpu.VMEM((images, rows // 4 + 2, 32, 128), jnp.float32),
    ]


def filtered(source, response, cos, sin):
    kind = jnp.bfloat16
    row_real = mm(source, cos).astype(kind)
    row_imag = (-mm(source, sin)).astype(kind)
    gain = 1.0 / (1.0 + response)
    spec_real = ((mm(cos, row_real) + mm(sin, row_imag)) * gain).astype(kind)
    spec_imag = ((mm(cos, row_imag) - mm(sin, row_real)) * gain).astype(kind)
    back_real = (mm(cos, spec_real) - mm(sin, spec_imag)).astype(kind)
    back_imag = (mm(cos, spec_imag) + mm(sin, spec_real)).astype(kind)
    return (mm(back_real, cos) - mm(back_imag, sin)) * (1.0 / (source.shape[0] * source.shape[1]))


def whole_kernel(depth, states, measured, response, cosine, sines, *rest):
    params, tables, spread, gather, out = rest[:5], rest[5:7], rest[7], rest[8], rest[9]
    built = [rest[10:16], rest[16:22], rest[22:28]]
    z_work, xy_work = rest[28:31], rest[31:34]
    z_own, z_other, turned, data, z_res, leaving, arrived, going, returned = rest[34:43]
    z_send, z_recv, there_send, there_recv, back_send, back_recv = rest[43:]
    kind = jnp.bfloat16
    devices = 2 * depth
    frame = lax.axis_index("frame")
    plane = lax.axis_index("plane")
    me = frame * depth + plane

    def at(k):
        other = me ^ k
        return other, (other // depth, other % depth)

    barrier = pltpu.get_barrier_semaphore()

    def greet(k, carry):
        pl.semaphore_signal(barrier, inc=1, device_id=at(k)[1], device_id_type=MESH)
        return carry

    lax.fori_loop(1, devices, greet, 0, unroll=UNROLL)

    z_own[...] = states[1].astype(kind)
    for which, value in enumerate((jnp.transpose(states[2]), states[3])):
        for half in range(2):
            turned[which * 2 + half] = value[:, half * 128:(half + 1) * 128]
        for p in range(2):
            for half in range(2):
                leaving[pl.ds(which * 4 + p * 2 + half, devices, stride=8), :] = turned[which * 2 + half, pl.ds(p, devices, stride=2), :]
    prepare(0, params, tables, built[0], 1)
    pl.semaphore_wait(barrier, devices - 1)

    def packet(ref, d):
        return ref.at[pl.ds(pl.multiple_of(d * 8, 8), 8), :]

    def exchange(source, target, send, recv):
        pltpu.make_async_copy(packet(source, me), packet(target, me), recv).start()

        def go(k, carry):
            other, coordinates = at(k)
            pltpu.make_async_remote_copy(
                src_ref=packet(source, other),
                dst_ref=packet(target, me),
                send_sem=send,
                recv_sem=recv,
                device_id=coordinates,
                device_id_type=MESH,
            ).start()
            return carry

        lax.fori_loop(1, devices, go, 0, unroll=UNROLL)

    def all_sent(source, send):
        some = source.at[pl.ds(0, (devices - 1) * 8), :]
        pltpu.make_async_copy(some, some, send).wait()

    def all_here(target, recv):
        pltpu.make_async_copy(target, target, recv).wait()

    swap = pltpu.make_async_remote_copy(
        src_ref=z_own, dst_ref=z_other, send_sem=z_send, recv_sem=z_recv,
        device_id=(1 - frame, plane), device_id_type=MESH,
    )
    swap.start()
    exchange(leaving, arrived, there_send, there_recv)

    prepare(1, params, tables, built[1], 2)
    prepare(2, params, tables, built[2], 2)
    source = (measured[...] + states[0]).astype(kind)
    data[...] = filtered(source, response[...], cosine[...], sines[...])
    swap.wait()
    first_half([(lambda: z_own[...], lambda: z_other[...])], built[0], spread[...], *z_work, frames=1)

    all_here(arrived, there_recv)
    all_sent(leaving, there_send)

    def rows_of(which, p, f, half):
        return pl.ds(f * depth * 8 + which * 4 + p * 2 + half, depth, stride=8)

    for which in range(2):

        def plane_of(p, f):
            return jnp.concatenate([arrived[rows_of(which, p, f, half), :] for half in range(2)], 1).astype(kind)

        def emit(p, f, value):
            for half in range(2):
                going[rows_of(which, p, f, half), :] = value[:, half * 128:(half + 1) * 128]

        pairs = [(functools.partial(plane_of, p, 0), functools.partial(plane_of, p, 1)) for p in range(2)]
        first_half(pairs, built[which + 1], spread[...], *xy_work, frames=2)
        second_half(built[which + 1], gather[...], emit, *xy_work[1:], frames=2)
    exchange(going, returned, back_send, back_recv)

    def emit_z(p, f, value):
        z_res[...] = value

    second_half(built[0], gather[...], emit_z, *z_work[1:], frames=1)
    all_here(returned, back_recv)
    all_sent(going, back_send)

    def unpack(which):
        for p in range(2):
            for half in range(2):
                turned[which * 2 + half, pl.ds(p, devices, stride=2), :] = returned[pl.ds(which * 4 + p * 2 + half, devices, stride=8), :]
        return jnp.concatenate([turned[which * 2], turned[which * 2 + 1]], 1)

    res_x = jnp.transpose(unpack(0))
    res_y = unpack(1)
    w = [states[k] for k in range(4)]
    z = [2.0 * data[...] - w[0], w[1] - 2.0 * z_res[...], w[2] - 2.0 * res_x, w[3] - 2.0 * res_y]
    twice = 0.5 * (z[0] + z[1] + z[2] + z[3])
    for k in range(4):
        out[k] = (1.0 - relaxation) * w[k] + relaxation * (twice - z[k])


def fourier_tables(length):
    indices = np.arange(length, dtype=np.int32)
    phase = indices[:, None] * indices[None, :] % length
    angle = phase.astype(np.float32) * np.float32(2.0 * math.pi / length)
    return (jnp.asarray(np.cos(angle), jnp.bfloat16), jnp.asarray(np.sin(angle), jnp.bfloat16))


def constants(width):
    kind = jnp.bfloat16
    tables = (first_table(), last_table(), spread_table(width), gather_table(width))
    return tuple(jnp.asarray(table.astype(kind)) for table in tables)


def on_device(states, measured, response, kernel_in, bias_in, kernel_mid, bias_mid, kernel_out):
    current = states[:, 0, 0]
    width = current.shape[-1]
    depth = lax.axis_size("plane")
    args = (current, measured[0, 0], response) + fourier_tables(width)
    args += (kernel_in, bias_in, kernel_mid, bias_mid, kernel_out) + constants(width)
    image = pltpu.VMEM((width, width), jnp.float32)
    short = pltpu.VMEM((width, width), jnp.bfloat16)
    packets = pltpu.VMEM((2 * depth * 8, 128), jnp.float32)
    out = pl.pallas_call(
        functools.partial(whole_kernel, depth),
        out_shape=jax.ShapeDtypeStruct(current.shape, jnp.float32),
        in_specs=[pl.BlockSpec(memory_space=pltpu.VMEM)] * len(args),
        out_specs=pl.BlockSpec(memory_space=pltpu.VMEM),
        scratch_shapes=built_shapes(1) + built_shapes(2) + built_shapes(2)
        + work_shapes(1, 1, width) + work_shapes(2, 2, depth)
        + [short, short, pltpu.VMEM((4, width, 128), jnp.float32), image, image, packets, packets, packets, packets]
        + [pltpu.SemaphoreType.DMA] * 6,
        compiler_params=pltpu.CompilerParams(vmem_limit_bytes=60 * 2**20, collective_id=0, has_side_effects=True),
        cost_estimate=pl.CostEstimate(flops=12 * 10**9, bytes_accessed=2**22, transcendentals=0),
    )(*args)
    return out[:, None, None]


def solution(mesh):
    placed = (
        P(None, "frame", "plane", None, None),
        P("frame", "plane", None, None),
        P(),
        P(),
        P(),
        P(),
        P(),
        P(),
    )
    return jax.shard_map(
        on_device,
        mesh=mesh,
        in_specs=placed,
        out_specs=P(None, "frame", "plane", None, None),
        check_vma=False,
    )
```

```python
import functools
import math

import jax
import jax.numpy as jnp
import numpy as np
from jax import lax
from jax.experimental import pallas as pl
from jax.experimental.pallas import tpu as pltpu
from jax.sharding import PartitionSpec as P

relaxation = 0.8
MESH = pl.DeviceIdType.MESH
UNROLL = 8

GROUPS = [(0, 0), (0, 1), (3, 0), (3, 1), (1, 0), (1, 1), (2, 0), (2, 1)]
STRIP = 16
FIRST_STEP = 8
MID_STEP = 16


def block_order(width):
    blocks = width // 2
    per = blocks // STRIP
    lane = np.arange(blocks)
    return (lane % STRIP) * per + lane // STRIP


def spread_table(width):
    blocks = width // 2
    order = block_order(width)
    table = np.zeros((width, 4 * blocks), np.float32)
    for xo in range(4):
        for lane in range(blocks):
            col = 2 * order[lane] + xo - 1
            if 0 <= col < width:
                table[col, xo * blocks + lane] = 1
    return table


def gather_table(width):
    blocks = width // 2
    order = block_order(width)
    table = np.zeros((width, width), np.float32)
    for j in range(2):
        for lane in range(blocks):
            table[j * blocks + lane, 2 * order[lane] + j] = 1
    return table


def select_in():
    chosen = np.zeros((9, 4, 24, 2, 8), np.float32)
    for half in range(2):
        for g, (i, j) in enumerate(GROUPS):
            for p in range(3):
                for q in range(3):
                    chosen[3 * p + q, j + q, 7 + 4 * half + i + p, half, g] = 1
    return chosen.reshape(9, 96, 16)


def slots_mid():
    slots = list(GROUPS)
    slots += [(i, -1 if j == 1 else 2) for i, j in GROUPS]
    slots += [(-1 if i == 3 else 4, j) for i, j in GROUPS[:4]]
    slots += [(-1 if i == 3 else 4, -1 if j == 1 else 2) for i, j in GROUPS[:4]]
    return slots


def select_mid():
    chosen = np.zeros((9, 24, 8), np.float32)
    for s, (row, col) in enumerate(slots_mid()):
        for g, (i, j) in enumerate(GROUPS):
            p, q = row - i + 1, col - j + 1
            if 0 <= p < 3 and 0 <= q < 3:
                chosen[3 * p + q, s, g] = 1
    return chosen


def select_out():
    targets = [None] * 32
    for j in range(2):
        far = 2 if j == 0 else -1
        for i in range(4):
            targets[j * 4 + i] = (i, j)
            targets[8 + j * 4 + i] = (i, far)
        for base, col in ((16, j), (24, far)):
            targets[base + j * 4] = (4, col)
            targets[base + j * 4 + 3] = (-1, col)
    chosen = np.zeros((9, 32, 8), np.float32)
    for r, target in enumerate(targets):
        if target is None:
            continue
        for g, (i, j) in enumerate(GROUPS):
            p, q = i - target[0] + 1, j - target[1] + 1
            if 0 <= p < 3 and 0 <= q < 3:
                chosen[3 * p + q, r, g] = 1
    return chosen


def first_table():
    chosen = select_in()
    table = np.zeros((2, 96, 16, 32), np.float32)
    for ch in range(2):
        for tap in range(9):
            table[ch, :, :, 2 * tap + ch] = chosen[tap]
    return table.reshape(192, 512)


def last_table():
    table = np.zeros((32, 8, 16), np.float32)
    table[:, :, :9] = select_out().transpose(1, 2, 0)
    return table.reshape(32, 128)


def mm(a, b, dims=((1,), (0,))):
    return lax.dot_general(a, b, (dims, ((), ())), preferred_element_type=jnp.float32)


def prepare(d, params, tables, built, frames):
    kernel_in, bias_in, kernel_mid, bias_mid, kernel_out = params
    first_at, last_at = tables
    w_first, b_first, w_mid, b_mid, w_last, spare = built
    kind = jnp.bfloat16
    lane = lax.broadcasted_iota(jnp.int32, (32, 512), 1)
    row = lax.broadcasted_iota(jnp.int32, (32, 512), 0)
    repeat = (lane % 32 == row).astype(jnp.float32)
    wide = repeat.astype(kind)
    narrow = wide[:, :256]

    spare[...] = jnp.zeros_like(spare)
    for tap in range(9):
        spare[2 * tap:2 * tap + 2, :] = mm(kernel_in[d, tap], wide)
    tiled = jnp.concatenate([spare[...]] * 16, 0)
    own = lax.broadcasted_iota(jnp.int32, (512, 512), 0) // 32 == lax.broadcasted_iota(jnp.int32, (512, 512), 1) // 32
    built_first = mm(first_at[...], jnp.where(own, tiled, 0.0).astype(kind)).astype(kind)
    w_first[:, 0:512] = built_first
    exact = lax.dot_general(bias_in[...], repeat, (((1,), (0,)), ((), ())), precision=lax.Precision.HIGHEST, preferred_element_type=jnp.float32)
    b_first[0:1, 0:512] = exact[d:d + 1]
    if frames == 2:
        w_first[0:96, 512:1024] = built_first[96:192]
        w_first[96:192, 512:1024] = built_first[0:96]
        b_first[0:1, 512:1024] = exact[d:d + 1]
    exact = lax.dot_general(bias_mid[:, 0, :], repeat[:, :256], (((1,), (0,)), ((), ())), precision=lax.Precision.HIGHEST, preferred_element_type=jnp.float32)
    b_mid[0:1, :] = exact[d:d + 1]

    taps = [mm(kernel_mid[d, 0, tap], narrow, ((0,), (0,))) for tap in range(9)]
    group = lane[:, :256] // 32
    for s, (r, c) in enumerate(slots_mid()):
        value = jnp.zeros((32, 256), jnp.float32)
        for g, (i, j) in enumerate(GROUPS):
            p, q = r - i + 1, c - j + 1
            if 0 <= p < 3 and 0 <= q < 3:
                value = jnp.where(group == g, taps[3 * p + q], value)
        w_mid[s * 32:(s + 1) * 32, :] = value.astype(kind)

    spare[9:16, 0:256] = jnp.zeros((7, 256), jnp.float32)
    spare[0:9, 0:256] = mm(kernel_out[:, d, :], narrow)
    tiled = jnp.concatenate([spare[0:16, 0:256]] * 8, 0)
    own = lax.broadcasted_iota(jnp.int32, (128, 256), 0) // 16 == lax.broadcasted_iota(jnp.int32, (128, 256), 1) // 32
    w_last[...] = mm(last_at[...], jnp.where(own, tiled, 0.0).astype(kind)).astype(kind)


def first_half(x, built, spread, u_ref, h_ref, c_ref, frames):
    w_first, b_first = built[:2]
    rows = u_ref.shape[1] - 16
    row_blocks = rows // 4
    images = len(x) * frames
    kind = jnp.bfloat16
    for pair in range(len(x)):
        for ch in range(2):
            u_ref[pair * 2 + ch, :8, :] = jnp.zeros((8, 512), jnp.float32)
            u_ref[pair * 2 + ch, rows + 8:, :] = jnp.zeros((8, 512), jnp.float32)
            u_ref[pair * 2 + ch, 8:rows + 8, :] = mm(x[pair][ch](), spread)
    for img in range(images):
        h_ref[img, 0] = jnp.zeros((160, 256), kind)
        h_ref[img, row_blocks + 1] = jnp.zeros((160, 256), kind)
        c_ref[img, 0] = jnp.zeros((32, 128), jnp.float32)
        c_ref[img, row_blocks + 1] = jnp.zeros((32, 128), jnp.float32)

    strip = lax.broadcasted_iota(jnp.int32, (16, 256), 0)
    first_strip = strip == 0
    last_strip = strip == 15

    def first_layer(step, carry):
        for pair in range(len(x)):
            parts = []
            for ch in range(2):
                for xo in range(4):
                    parts.append(jnp.concatenate([
                        u_ref[pair * 2 + ch, pl.ds(pl.multiple_of((step * FIRST_STEP + k) * 8, 8), 24), xo * 128:(xo + 1) * 128]
                        for k in range(FIRST_STEP)], 1))
            stacked = jnp.concatenate(parts, 0).astype(kind)
            made = mm(stacked, w_first[...], ((0,), (0,)))
            made = jnp.maximum(made + b_first[0:1, :], 0.0)
            for f in range(frames):
                for k in range(FIRST_STEP):
                    for half in range(2):
                        at = f * 512 + half * 256
                        piece = made[k * 128:(k + 1) * 128, at:at + 256]
                        to = h_ref.at[pair * frames + f, 2 * (step * FIRST_STEP + k) + half + 1]
                        to[16:144, :] = piece.astype(kind)
                        to[0:16, :] = jnp.where(first_strip, 0.0, pltpu.roll(piece[112:128], 1, 0)).astype(kind)
                        to[144:160, :] = jnp.where(last_strip, 0.0, pltpu.roll(piece[0:16], 15, 0)).astype(kind)
        return carry

    lax.fori_loop(0, rows // 8 // FIRST_STEP, first_layer, 0)


def second_half(built, gather, emit, h_ref, c_ref, frames):
    w_mid, b_mid, w_last = built[2:5]
    images = h_ref.shape[0]
    row_blocks = h_ref.shape[1] - 2
    rows = row_blocks * 4
    kind = jnp.bfloat16
    n = MID_STEP * 128
    right = (lax.broadcasted_iota(jnp.int32, (n, 256), 1) // 32) % 2 == 1
    right_half = right[:, :128]
    low = lax.broadcasted_iota(jnp.int32, (n, 128), 1) >= 64
    steps = row_blocks // MID_STEP

    def mid_layer(at, carry):
        img, a = at // steps, (at % steps) * MID_STEP

        def part(down, shift, lanes):
            return h_ref[img, pl.ds(a + 1 + down, MID_STEP), 16 + shift:144 + shift, 0:lanes].reshape(n, lanes)

        here = part(0, 0, 256)
        side = jnp.where(right, part(0, -16, 256), part(0, 16, 256))
        across = jnp.where(low, part(-1, 0, 128), part(1, 0, 128))
        corner_left = jnp.where(low, part(-1, -16, 128), part(1, -16, 128))
        corner_right = jnp.where(low, part(-1, 16, 128), part(1, 16, 128))
        corner = jnp.where(right_half, corner_left, corner_right)
        made = mm(jnp.concatenate([here, side, across, corner], 1), w_mid[...])
        hidden = jnp.maximum(made + b_mid[0:1, :], 0.0).astype(kind)
        last = mm(w_last[...], hidden, ((1,), (1,)))
        for k in range(MID_STEP):
            c_ref[img, a + 1 + k] = last[:, k * 128:(k + 1) * 128]
        return carry

    lax.fori_loop(0, images * steps, mid_layer, 0)

    lane = lax.broadcasted_iota(jnp.int32, (row_blocks * 8, 128), 1)
    sub = lax.broadcasted_iota(jnp.int32, (row_blocks * 8, 128), 0) % 8
    half_sub = sub[:row_blocks * 4]

    def moved(value):
        before = jnp.where(lane >= 16, pltpu.roll(value, 16, 1), jnp.where(lane >= 1, pltpu.roll(value, 17, 1), 0.0))
        after = jnp.where(lane < 112, pltpu.roll(value, 112, 1), jnp.where(lane < 127, pltpu.roll(value, 111, 1), 0.0))
        return jnp.where(sub < 4, before, after)

    for img in range(images):

        def piece(at, down=0):
            return c_ref[img, 1 + down:1 + down + row_blocks, at:at + 8, :].reshape(row_blocks * 8, 128)

        total = piece(0) + moved(piece(8))
        edges = piece(16) + moved(piece(24))
        c_ref[img, 1:1 + row_blocks, 16:24, :] = edges.reshape(row_blocks, 8, 128)
        total += jnp.where(sub % 4 == 0, piece(16, -1), 0.0) + jnp.where(sub % 4 == 3, piece(16, 1), 0.0)
        twos = total.reshape(row_blocks // 2, 16, 128)
        even = twos[:, 0:8].reshape(row_blocks * 4, 128)
        odd = twos[:, 8:16].reshape(row_blocks * 4, 128)
        left = jnp.where(half_sub < 4, even, pltpu.roll(odd, 4, 0))
        right_side = jnp.where(half_sub < 4, pltpu.roll(even, rows - 4, 0), odd)
        emit(img // frames, img % frames, mm(jnp.concatenate([left, right_side], 1).astype(kind), gather))


def built_shapes(frames):
    return [
        pltpu.VMEM((192, frames * 512), jnp.bfloat16),
        pltpu.VMEM((8, frames * 512), jnp.float32),
        pltpu.VMEM((768, 256), jnp.bfloat16),
        pltpu.VMEM((8, 256), jnp.float32),
        pltpu.VMEM((32, 256), jnp.bfloat16),
        pltpu.VMEM((32, 512), jnp.float32),
    ]


def work_shapes(pairs, frames, rows):
    images = pairs * frames
    return [
        pltpu.VMEM((pairs * 2, rows + 16, 512), jnp.float32),
        pltpu.VMEM((images, rows // 4 + 2, 160, 256), jnp.bfloat16),
        pltpu.VMEM((images, rows // 4 + 2, 32, 128), jnp.float32),
    ]


def filtered(source, response, cos, sin):
    kind = jnp.bfloat16
    row_real = mm(source, cos).astype(kind)
    row_imag = (-mm(source, sin)).astype(kind)
    gain = 1.0 / (1.0 + response)
    spec_real = ((mm(cos, row_real) + mm(sin, row_imag)) * gain).astype(kind)
    spec_imag = ((mm(cos, row_imag) - mm(sin, row_real)) * gain).astype(kind)
    back_real = (mm(cos, spec_real) - mm(sin, spec_imag)).astype(kind)
    back_imag = (mm(cos, spec_imag) + mm(sin, spec_real)).astype(kind)
    return (mm(back_real, cos) - mm(back_imag, sin)) * (1.0 / (source.shape[0] * source.shape[1]))


def whole_kernel(depth, states_at, measured_at, response_at, cosine_at, sines_at, *rest):
    params, tables, spread, gather = rest[:5], rest[5:7], rest[7], rest[8]
    data, z_res, x_res, y_res = rest[9:13]
    rest = rest[13:]
    built = [rest[0:6], rest[6:12], rest[12:18]]
    z_work, xy_work = rest[18:21], rest[21:24]
    z_own, z_other, turned, rows_f32, leaving, arrived, going, returned = rest[24:32]
    states, measured, response, cosine, sines, loaded = rest[32:38]
    z_send, z_recv, there_send, there_recv, back_send, back_recv = rest[38:]
    kind = jnp.bfloat16
    devices = 2 * depth
    frame = lax.axis_index("frame")
    plane = lax.axis_index("plane")
    me = frame * depth + plane

    def at(k):
        other = me ^ k
        return other, (other // depth, other % depth)

    barrier = pltpu.get_barrier_semaphore()

    def greet(k, carry):
        pl.semaphore_signal(barrier, inc=1, device_id=at(k)[1], device_id_type=MESH)
        return carry

    loads = [pltpu.make_async_copy(states_at.at[k], states.at[k], loaded.at[k]) for k in range(4)]
    for k, (source, target) in enumerate(((measured_at, measured), (response_at, response), (cosine_at, cosine), (sines_at, sines))):
        loads.append(pltpu.make_async_copy(source, target, loaded.at[4 + k]))
    for k in (2, 3, 1, 0, 4, 5, 6, 7):
        loads[k].start()
    lax.fori_loop(1, devices, greet, 0, unroll=UNROLL)

    loads[2].wait()
    loads[3].wait()
    for which, value in enumerate((jnp.transpose(states[2]), states[3])):
        for half in range(2):
            turned[which * 2 + half] = value[:, half * 128:(half + 1) * 128]
        for p in range(2):
            for half in range(2):
                rows_f32[pl.ds(which * 4 + p * 2 + half, devices, stride=8), :] = turned[which * 2 + half, pl.ds(p, devices, stride=2), :]
    leaving[...] = rows_f32[...].reshape(devices, 8, 128).astype(kind)
    loads[1].wait()
    z_own[...] = states[1].astype(kind)
    prepare(0, params, tables, built[0], 1)
    pl.semaphore_wait(barrier, devices - 1)

    def packet(ref, d):
        return ref.at[d]

    def exchange(source, target, send, recv):
        pltpu.make_async_copy(packet(source, me), packet(target, me), recv).start()

        def go(k, carry):
            other, coordinates = at(k)
            pltpu.make_async_remote_copy(
                src_ref=packet(source, other),
                dst_ref=packet(target, me),
                send_sem=send,
                recv_sem=recv,
                device_id=coordinates,
                device_id_type=MESH,
            ).start()
            return carry

        lax.fori_loop(1, devices, go, 0, unroll=UNROLL)

    def all_sent(source, send):
        some = source.at[pl.ds(0, devices - 1)]
        pltpu.make_async_copy(some, some, send).wait()

    def all_here(target, recv):
        pltpu.make_async_copy(target, target, recv).wait()

    swap = pltpu.make_async_remote_copy(
        src_ref=z_own, dst_ref=z_other, send_sem=z_send, recv_sem=z_recv,
        device_id=(1 - frame, plane), device_id_type=MESH,
    )
    swap.start()
    exchange(leaving, arrived, there_send, there_recv)

    prepare(1, params, tables, built[1], 2)
    prepare(2, params, tables, built[2], 2)
    for k in (0, 4, 5, 6, 7):
        loads[k].wait()
    source = (measured[...] + states[0]).astype(kind)
    data[...] = filtered(source, response[...], cosine[...], sines[...])
    swap.wait()
    first_half([(lambda: z_own[...], lambda: z_other[...])], built[0], spread[...], *z_work, frames=1)

    all_here(arrived, there_recv)
    all_sent(leaving, there_send)
    rows_f32[...] = arrived[...].astype(jnp.float32).reshape(devices * 8, 128)

    def rows_of(which, p, f, half):
        return pl.ds(f * depth * 8 + which * 4 + p * 2 + half, depth, stride=8)

    for which in range(2):

        def plane_of(p, f):
            return jnp.concatenate([rows_f32[rows_of(which, p, f, half), :] for half in range(2)], 1).astype(kind)

        def emit(p, f, value):
            for half in range(2):
                rows_f32[rows_of(which, p, f, half), :] = value[:, half * 128:(half + 1) * 128]

        pairs = [(functools.partial(plane_of, p, 0), functools.partial(plane_of, p, 1)) for p in range(2)]
        first_half(pairs, built[which + 1], spread[...], *xy_work, frames=2)
        second_half(built[which + 1], gather[...], emit, *xy_work[1:], frames=2)
    going[...] = rows_f32[...].reshape(devices, 8, 128).astype(kind)
    exchange(going, returned, back_send, back_recv)

    def emit_z(p, f, value):
        z_res[...] = value.astype(kind)

    second_half(built[0], gather[...], emit_z, *z_work[1:], frames=1)
    all_here(returned, back_recv)
    all_sent(going, back_send)

    rows_f32[...] = returned[...].astype(jnp.float32).reshape(devices * 8, 128)

    def unpack(which):
        for p in range(2):
            for half in range(2):
                turned[which * 2 + half, pl.ds(p, devices, stride=2), :] = rows_f32[pl.ds(which * 4 + p * 2 + half, devices, stride=8), :]
        return jnp.concatenate([turned[which * 2], turned[which * 2 + 1]], 1)

    x_res[...] = jnp.transpose(unpack(0)).astype(kind)
    y_res[...] = unpack(1).astype(kind)


def final_kernel(states, data, res_z, res_x, res_y, out):
    w = [states[k] for k in range(4)]
    z = [2.0 * data[...] - w[0]]
    z += [w[k + 1] - 2.0 * res[...].astype(jnp.float32) for k, res in enumerate((res_z, res_x, res_y))]
    twice = 0.5 * (z[0] + z[1] + z[2] + z[3])
    for k in range(4):
        out[k] = (1.0 - relaxation) * w[k] + relaxation * (twice - z[k])


def fourier_tables(length):
    indices = np.arange(length, dtype=np.int32)
    phase = indices[:, None] * indices[None, :] % length
    angle = phase.astype(np.float32) * np.float32(2.0 * math.pi / length)
    return (jnp.asarray(np.cos(angle), jnp.bfloat16), jnp.asarray(np.sin(angle), jnp.bfloat16))


def constants(width):
    kind = jnp.bfloat16
    tables = (first_table(), last_table(), spread_table(width), gather_table(width))
    return tuple(jnp.asarray(table.astype(kind)) for table in tables)


def on_device(states, measured, response, kernel_in, bias_in, kernel_mid, bias_mid, kernel_out):
    current = states[:, 0, 0]
    width = current.shape[-1]
    depth = lax.axis_size("plane")
    kind = jnp.bfloat16
    args = (current, measured[0, 0], response) + fourier_tables(width)
    args += (jnp.transpose(kernel_in, (0, 1, 3, 2)), bias_in, kernel_mid, bias_mid, jnp.transpose(kernel_out, (1, 0, 2))) + constants(width)
    short = pltpu.VMEM((width, width), kind)
    image = pltpu.VMEM((width, width), jnp.float32)
    packets = pltpu.VMEM((2 * depth, 8, 128), kind)
    sharp = jax.ShapeDtypeStruct((width, width), jnp.float32)
    coarse = jax.ShapeDtypeStruct((width, width), kind)
    found = pl.pallas_call(
        functools.partial(whole_kernel, depth),
        out_shape=(sharp, coarse, coarse, coarse),
        in_specs=[pl.BlockSpec(memory_space=pl.ANY)] * 5 + [pl.BlockSpec(memory_space=pltpu.VMEM)] * (len(args) - 5),
        out_specs=(pl.BlockSpec(memory_space=pltpu.VMEM),) * 4,
        scratch_shapes=built_shapes(1) + built_shapes(2) + built_shapes(2)
        + work_shapes(1, 1, width) + work_shapes(2, 2, depth)
        + [short, short, pltpu.VMEM((4, width, 128), jnp.float32), pltpu.VMEM((2 * depth * 8, 128), jnp.float32)]
        + [packets] * 4
        + [pltpu.VMEM((4, width, width), jnp.float32), image, image, short, short, pltpu.SemaphoreType.DMA((8,))]
        + [pltpu.SemaphoreType.DMA] * 6,
        compiler_params=pltpu.CompilerParams(vmem_limit_bytes=60 * 2**20, collective_id=0, has_side_effects=True),
        cost_estimate=pl.CostEstimate(flops=12 * 10**9, bytes_accessed=2**22, transcendentals=0),
    )(*args)
    step = width // 4
    flat = pl.BlockSpec((step, width), lambda i: (i, 0))
    deep = pl.BlockSpec((4, step, width), lambda i: (0, i, 0))
    out = pl.pallas_call(
        final_kernel,
        grid=(4,),
        out_shape=jax.ShapeDtypeStruct(current.shape, jnp.float32),
        in_specs=[deep, flat, flat, flat, flat],
        out_specs=deep,
        cost_estimate=pl.CostEstimate(flops=2 * 10**6, bytes_accessed=2**21, transcendentals=0),
    )(current, *found)
    return out[:, None, None]


def solution(mesh):
    placed = (
        P(None, "frame", "plane", None, None),
        P("frame", "plane", None, None),
        P(),
        P(),
        P(),
        P(),
        P(),
        P(),
    )
    return jax.shard_map(
        on_device,
        mesh=mesh,
        in_specs=placed,
        out_specs=P(None, "frame", "plane", None, None),
        check_vma=False,
    )
```

```python
import functools
import math

import jax
import jax.numpy as jnp
import numpy as np
from jax import lax
from jax.experimental import pallas as pl
from jax.experimental.pallas import tpu as pltpu
from jax.sharding import PartitionSpec as P

relaxation = 0.8
MESH = pl.DeviceIdType.MESH
UNROLL = 8

GROUPS = [(0, 0), (0, 1), (3, 0), (3, 1), (1, 0), (1, 1), (2, 0), (2, 1)]
STRIP = 16
FIRST_STEP = 8
MID_STEP = 16


def block_order(width):
    blocks = width // 2
    per = blocks // STRIP
    lane = np.arange(blocks)
    return (lane % STRIP) * per + lane // STRIP


def spread_table(width):
    blocks = width // 2
    order = block_order(width)
    table = np.zeros((width, 4 * blocks), np.float32)
    for xo in range(4):
        for lane in range(blocks):
            col = 2 * order[lane] + xo - 1
            if 0 <= col < width:
                table[col, xo * blocks + lane] = 1
    return table


def gather_table(width):
    blocks = width // 2
    order = block_order(width)
    table = np.zeros((width, width), np.float32)
    for j in range(2):
        for lane in range(blocks):
            table[j * blocks + lane, 2 * order[lane] + j] = 1
    return table


def select_in():
    chosen = np.zeros((9, 4, 24, 2, 8), np.float32)
    for half in range(2):
        for g, (i, j) in enumerate(GROUPS):
            for p in range(3):
                for q in range(3):
                    chosen[3 * p + q, j + q, 7 + 4 * half + i + p, half, g] = 1
    return chosen.reshape(9, 96, 16)


def slots_mid():
    slots = list(GROUPS)
    slots += [(i, -1 if j == 1 else 2) for i, j in GROUPS]
    slots += [(-1 if i == 3 else 4, j) for i, j in GROUPS[:4]]
    slots += [(-1 if i == 3 else 4, -1 if j == 1 else 2) for i, j in GROUPS[:4]]
    return slots


def select_mid():
    chosen = np.zeros((9, 24, 8), np.float32)
    for s, (row, col) in enumerate(slots_mid()):
        for g, (i, j) in enumerate(GROUPS):
            p, q = row - i + 1, col - j + 1
            if 0 <= p < 3 and 0 <= q < 3:
                chosen[3 * p + q, s, g] = 1
    return chosen


def select_out():
    targets = [None] * 32
    for j in range(2):
        far = 2 if j == 0 else -1
        for i in range(4):
            targets[j * 4 + i] = (i, j)
            targets[8 + j * 4 + i] = (i, far)
        for base, col in ((16, j), (24, far)):
            targets[base + j * 4] = (4, col)
            targets[base + j * 4 + 3] = (-1, col)
    chosen = np.zeros((9, 32, 8), np.float32)
    for r, target in enumerate(targets):
        if target is None:
            continue
        for g, (i, j) in enumerate(GROUPS):
            p, q = i - target[0] + 1, j - target[1] + 1
            if 0 <= p < 3 and 0 <= q < 3:
                chosen[3 * p + q, r, g] = 1
    return chosen


def first_table():
    chosen = select_in()
    table = np.zeros((2, 96, 16, 32), np.float32)
    for ch in range(2):
        for tap in range(9):
            table[ch, :, :, 2 * tap + ch] = chosen[tap]
    return table.reshape(192, 512)


def last_table():
    table = np.zeros((32, 8, 16), np.float32)
    table[:, :, :9] = select_out().transpose(1, 2, 0)
    return table.reshape(32, 128)


def mm(a, b, dims=((1,), (0,))):
    return lax.dot_general(a, b, (dims, ((), ())), preferred_element_type=jnp.float32)


def prepare(d, params, tables, built, frames):
    kernel_in, bias_in, kernel_mid, bias_mid, kernel_out = params
    first_at, last_at = tables
    w_first, b_first, w_mid, b_mid, w_last, spare = built
    kind = jnp.bfloat16
    lane = lax.broadcasted_iota(jnp.int32, (32, 512), 1)
    row = lax.broadcasted_iota(jnp.int32, (32, 512), 0)
    repeat = (lane % 32 == row).astype(jnp.float32)
    wide = repeat.astype(kind)
    narrow = wide[:, :256]

    spare[...] = jnp.zeros_like(spare)
    for tap in range(9):
        spare[2 * tap:2 * tap + 2, :] = mm(kernel_in[d, tap], wide)
    tiled = jnp.concatenate([spare[...]] * 16, 0)
    own = lax.broadcasted_iota(jnp.int32, (512, 512), 0) // 32 == lax.broadcasted_iota(jnp.int32, (512, 512), 1) // 32
    built_first = mm(first_at[...], jnp.where(own, tiled, 0.0).astype(kind)).astype(kind)
    w_first[:, 0:512] = built_first
    exact = lax.dot_general(bias_in[...], repeat, (((1,), (0,)), ((), ())), precision=lax.Precision.HIGHEST, preferred_element_type=jnp.float32)
    b_first[0:1, 0:512] = exact[d:d + 1]
    if frames == 2:
        w_first[0:96, 512:1024] = built_first[96:192]
        w_first[96:192, 512:1024] = built_first[0:96]
        b_first[0:1, 512:1024] = exact[d:d + 1]
    exact = lax.dot_general(bias_mid[:, 0, :], repeat[:, :256], (((1,), (0,)), ((), ())), precision=lax.Precision.HIGHEST, preferred_element_type=jnp.float32)
    b_mid[0:1, :] = exact[d:d + 1]

    taps = [mm(kernel_mid[d, 0, tap], narrow, ((0,), (0,))) for tap in range(9)]
    group = lane[:, :256] // 32
    for s, (r, c) in enumerate(slots_mid()):
        value = jnp.zeros((32, 256), jnp.float32)
        for g, (i, j) in enumerate(GROUPS):
            p, q = r - i + 1, c - j + 1
            if 0 <= p < 3 and 0 <= q < 3:
                value = jnp.where(group == g, taps[3 * p + q], value)
        w_mid[s * 32:(s + 1) * 32, :] = value.astype(kind)

    spare[9:16, 0:256] = jnp.zeros((7, 256), jnp.float32)
    spare[0:9, 0:256] = mm(kernel_out[:, d, :], narrow)
    tiled = jnp.concatenate([spare[0:16, 0:256]] * 8, 0)
    own = lax.broadcasted_iota(jnp.int32, (128, 256), 0) // 16 == lax.broadcasted_iota(jnp.int32, (128, 256), 1) // 32
    w_last[...] = mm(last_at[...], jnp.where(own, tiled, 0.0).astype(kind)).astype(kind)


def first_half(x, built, spread, u_ref, h_ref, c_ref, frames):
    w_first, b_first = built[:2]
    rows = u_ref.shape[1] - 16
    row_blocks = rows // 4
    images = len(x) * frames
    kind = jnp.bfloat16
    for pair in range(len(x)):
        for ch in range(2):
            u_ref[pair * 2 + ch, :8, :] = jnp.zeros((8, 512), jnp.float32)
            u_ref[pair * 2 + ch, rows + 8:, :] = jnp.zeros((8, 512), jnp.float32)
            u_ref[pair * 2 + ch, 8:rows + 8, :] = mm(x[pair][ch](), spread)
    for img in range(images):
        h_ref[img, 0] = jnp.zeros((160, 256), kind)
        h_ref[img, row_blocks + 1] = jnp.zeros((160, 256), kind)
        c_ref[img, 0] = jnp.zeros((32, 128), jnp.float32)
        c_ref[img, row_blocks + 1] = jnp.zeros((32, 128), jnp.float32)

    strip = lax.broadcasted_iota(jnp.int32, (16, 256), 0)
    first_strip = strip == 0
    last_strip = strip == 15

    def first_layer(step, carry):
        for pair in range(len(x)):
            parts = []
            for ch in range(2):
                for xo in range(4):
                    parts.append(jnp.concatenate([
                        u_ref[pair * 2 + ch, pl.ds(pl.multiple_of((step * FIRST_STEP + k) * 8, 8), 24), xo * 128:(xo + 1) * 128]
                        for k in range(FIRST_STEP)], 1))
            stacked = jnp.concatenate(parts, 0).astype(kind)
            made = mm(stacked, w_first[...], ((0,), (0,)))
            made = jnp.maximum(made + b_first[0:1, :], 0.0)
            for f in range(frames):
                for k in range(FIRST_STEP):
                    for half in range(2):
                        at = f * 512 + half * 256
                        piece = made[k * 128:(k + 1) * 128, at:at + 256]
                        to = h_ref.at[pair * frames + f, 2 * (step * FIRST_STEP + k) + half + 1]
                        to[16:144, :] = piece.astype(kind)
                        to[0:16, :] = jnp.where(first_strip, 0.0, pltpu.roll(piece[112:128], 1, 0)).astype(kind)
                        to[144:160, :] = jnp.where(last_strip, 0.0, pltpu.roll(piece[0:16], 15, 0)).astype(kind)
        return carry

    lax.fori_loop(0, rows // 8 // FIRST_STEP, first_layer, 0)


def second_half(built, gather, emit, h_ref, c_ref, frames, between=None):
    w_mid, b_mid, w_last = built[2:5]
    images = h_ref.shape[0]
    row_blocks = h_ref.shape[1] - 2
    rows = row_blocks * 4
    kind = jnp.bfloat16
    n = MID_STEP * 128
    right = (lax.broadcasted_iota(jnp.int32, (n, 256), 1) // 32) % 2 == 1
    right_half = right[:, :128]
    low = lax.broadcasted_iota(jnp.int32, (n, 128), 1) >= 64
    steps = row_blocks // MID_STEP

    def mid_layer(at, carry):
        img, a = at // steps, (at % steps) * MID_STEP

        def part(down, shift, lanes):
            return h_ref[img, pl.ds(a + 1 + down, MID_STEP), 16 + shift:144 + shift, 0:lanes].reshape(n, lanes)

        here = part(0, 0, 256)
        side = jnp.where(right, part(0, -16, 256), part(0, 16, 256))
        across = jnp.where(low, part(-1, 0, 128), part(1, 0, 128))
        corner_left = jnp.where(low, part(-1, -16, 128), part(1, -16, 128))
        corner_right = jnp.where(low, part(-1, 16, 128), part(1, 16, 128))
        corner = jnp.where(right_half, corner_left, corner_right)
        made = mm(jnp.concatenate([here, side, across, corner], 1), w_mid[...])
        hidden = jnp.maximum(made + b_mid[0:1, :], 0.0).astype(kind)
        last = mm(w_last[...], hidden, ((1,), (1,)))
        for k in range(MID_STEP):
            c_ref[img, a + 1 + k] = last[:, k * 128:(k + 1) * 128]
        return carry

    if between is None:
        lax.fori_loop(0, images * steps, mid_layer, 0)
    else:
        lax.fori_loop(0, 1, mid_layer, 0)
        between()
        lax.fori_loop(1, images * steps, mid_layer, 0)

    lane = lax.broadcasted_iota(jnp.int32, (row_blocks * 8, 128), 1)
    sub = lax.broadcasted_iota(jnp.int32, (row_blocks * 8, 128), 0) % 8
    half_sub = sub[:row_blocks * 4]

    def moved(value):
        before = jnp.where(lane >= 16, pltpu.roll(value, 16, 1), jnp.where(lane >= 1, pltpu.roll(value, 17, 1), 0.0))
        after = jnp.where(lane < 112, pltpu.roll(value, 112, 1), jnp.where(lane < 127, pltpu.roll(value, 111, 1), 0.0))
        return jnp.where(sub < 4, before, after)

    for img in range(images):

        def piece(at, down=0):
            return c_ref[img, 1 + down:1 + down + row_blocks, at:at + 8, :].reshape(row_blocks * 8, 128)

        total = piece(0) + moved(piece(8))
        edges = piece(16) + moved(piece(24))
        c_ref[img, 1:1 + row_blocks, 16:24, :] = edges.reshape(row_blocks, 8, 128)
        total += jnp.where(sub % 4 == 0, piece(16, -1), 0.0) + jnp.where(sub % 4 == 3, piece(16, 1), 0.0)
        twos = total.reshape(row_blocks // 2, 16, 128)
        even = twos[:, 0:8].reshape(row_blocks * 4, 128)
        odd = twos[:, 8:16].reshape(row_blocks * 4, 128)
        left = jnp.where(half_sub < 4, even, pltpu.roll(odd, 4, 0))
        right_side = jnp.where(half_sub < 4, pltpu.roll(even, rows - 4, 0), odd)
        emit(img // frames, img % frames, mm(jnp.concatenate([left, right_side], 1).astype(kind), gather))


def built_shapes(frames):
    return [
        pltpu.VMEM((192, frames * 512), jnp.bfloat16),
        pltpu.VMEM((8, frames * 512), jnp.float32),
        pltpu.VMEM((768, 256), jnp.bfloat16),
        pltpu.VMEM((8, 256), jnp.float32),
        pltpu.VMEM((32, 256), jnp.bfloat16),
        pltpu.VMEM((32, 512), jnp.float32),
    ]


def work_shapes(pairs, frames, rows):
    images = pairs * frames
    return [
        pltpu.VMEM((pairs * 2, rows + 16, 512), jnp.float32),
        pltpu.VMEM((images, rows // 4 + 2, 160, 256), jnp.bfloat16),
        pltpu.VMEM((images, rows // 4 + 2, 32, 128), jnp.float32),
    ]


def filtered(source, response, cos, sin):
    kind = jnp.bfloat16
    row_real = mm(source, cos).astype(kind)
    row_imag = (-mm(source, sin)).astype(kind)
    gain = 1.0 / (1.0 + response)
    spec_real = ((mm(cos, row_real) + mm(sin, row_imag)) * gain).astype(kind)
    spec_imag = ((mm(cos, row_imag) - mm(sin, row_real)) * gain).astype(kind)
    back_real = (mm(cos, spec_real) - mm(sin, spec_imag)).astype(kind)
    back_imag = (mm(cos, spec_imag) + mm(sin, spec_real)).astype(kind)
    return (mm(back_real, cos) - mm(back_imag, sin)) * (1.0 / (source.shape[0] * source.shape[1]))


def whole_kernel(depth, states_at, measured_at, response_at, cosine_at, sines_at, *rest):
    params, tables, spread, gather = rest[:5], rest[5:7], rest[7], rest[8]
    data, z_res, x_res, y_res = rest[9:13]
    rest = rest[13:]
    built = [rest[0:6], rest[6:12], rest[12:18]]
    z_work, xy_work = rest[18:21], rest[21:24]
    z_own, z_other, turned, rows_f32 = rest[24:28]
    there, back = rest[28:31], rest[31:34]
    states, measured, response, cosine, sines, loaded = rest[34:40]
    z_send, z_recv = rest[40:42]
    there_sems, back_sems = rest[42:47], rest[47:52]
    kind = jnp.bfloat16
    devices = 2 * depth
    frame = lax.axis_index("frame")
    plane = lax.axis_index("plane")
    chips = devices // 2
    chip = (frame * depth + plane) // 2
    core = (frame * depth + plane) % 2
    sibling = (frame, plane + 1 - 2 * core)

    def at(k):
        other = (chip ^ k) * 2 + core
        return chip ^ k, (other // depth, other % depth)

    barrier = pltpu.get_barrier_semaphore()

    def greet(k, carry):
        pl.semaphore_signal(barrier, inc=1, device_id=at(k)[1], device_id_type=MESH)
        return carry

    loads = [pltpu.make_async_copy(states_at.at[k], states.at[k], loaded.at[k]) for k in range(4)]
    for k, (source, target) in enumerate(((measured_at, measured), (response_at, response), (cosine_at, cosine), (sines_at, sines))):
        loads.append(pltpu.make_async_copy(source, target, loaded.at[4 + k]))
    for k in (2, 3, 1, 0, 4, 5, 6, 7):
        loads[k].start()
    pl.semaphore_signal(barrier, inc=1, device_id=sibling, device_id_type=MESH)
    lax.fori_loop(1, chips, greet, 0, unroll=UNROLL)

    def pack(buffer):
        value = rows_f32[...].astype(kind).reshape(chips, 2, 8, 128)
        buffer[0] = value[:, 0]
        buffer[1] = value[:, 1]

    def unpack_rows(buffer):
        rows_f32[...] = buffer[...].astype(jnp.float32).reshape(devices * 8, 128)

    def within_chip(buffers, sems):
        source, mixed, _ = buffers
        keep, send, recv, _, _ = sems
        moves = [
            pltpu.make_async_copy(source.at[core], mixed.at[:, core], keep),
            pltpu.make_async_remote_copy(
                src_ref=source.at[1 - core], dst_ref=mixed.at[:, core], send_sem=send, recv_sem=recv,
                device_id=sibling, device_id_type=MESH,
            ),
        ]
        for move in moves:
            move.start()
        return moves

    loads[2].wait()
    loads[3].wait()
    for which, value in enumerate((jnp.transpose(states[2]), states[3])):
        for half in range(2):
            turned[which * 2 + half] = value[:, half * 128:(half + 1) * 128]
        for p in range(2):
            for half in range(2):
                rows_f32[pl.ds(which * 4 + p * 2 + half, devices, stride=8), :] = turned[which * 2 + half, pl.ds(p, devices, stride=2), :]
    pack(there[0])
    loads[1].wait()
    z_own[...] = states[1].astype(kind)
    pl.semaphore_wait(barrier, chips)

    def between_chips(buffers, sems, moves):
        _, mixed, target = buffers
        _, _, _, send, recv = sems
        for move in moves:
            move.wait()
        pltpu.make_async_copy(mixed.at[chip], target.at[chip], recv).start()

        def go(k, carry):
            other, coordinates = at(k)
            pltpu.make_async_remote_copy(
                src_ref=mixed.at[other], dst_ref=target.at[chip], send_sem=send, recv_sem=recv,
                device_id=coordinates, device_id_type=MESH,
            ).start()
            return carry

        lax.fori_loop(1, chips, go, 0, unroll=UNROLL)

    def finish(buffers, sems):
        _, mixed, target = buffers
        pltpu.make_async_copy(target, target, sems[4]).wait()
        some = mixed.at[pl.ds(0, chips - 1)]
        pltpu.make_async_copy(some, some, sems[3]).wait()

    there_moves = within_chip(there, there_sems)
    swap = pltpu.make_async_remote_copy(
        src_ref=z_own, dst_ref=z_other, send_sem=z_send, recv_sem=z_recv,
        device_id=(1 - frame, plane), device_id_type=MESH,
    )
    swap.start()
    prepare(0, params, tables, built[0], 1)
    prepare(1, params, tables, built[1], 2)
    between_chips(there, there_sems, there_moves)
    prepare(2, params, tables, built[2], 2)
    for k in (0, 4, 5, 6, 7):
        loads[k].wait()
    source = (measured[...] + states[0]).astype(kind)
    data[...] = filtered(source, response[...], cosine[...], sines[...])
    swap.wait()
    first_half([(lambda: z_own[...], lambda: z_other[...])], built[0], spread[...], *z_work, frames=1)

    finish(there, there_sems)
    unpack_rows(there[2])

    def rows_of(which, p, f, half):
        return pl.ds(f * depth * 8 + which * 4 + p * 2 + half, depth, stride=8)

    for which in range(2):

        def plane_of(p, f):
            return jnp.concatenate([rows_f32[rows_of(which, p, f, half), :] for half in range(2)], 1).astype(kind)

        def emit(p, f, value):
            for half in range(2):
                rows_f32[rows_of(which, p, f, half), :] = value[:, half * 128:(half + 1) * 128]

        pairs = [(functools.partial(plane_of, p, 0), functools.partial(plane_of, p, 1)) for p in range(2)]
        first_half(pairs, built[which + 1], spread[...], *xy_work, frames=2)
        second_half(built[which + 1], gather[...], emit, *xy_work[1:], frames=2)
    pack(back[0])
    back_moves = within_chip(back, back_sems)

    def emit_z(p, f, value):
        z_res[...] = value.astype(kind)

    second_half(built[0], gather[...], emit_z, *z_work[1:], frames=1, between=lambda: between_chips(back, back_sems, back_moves))
    finish(back, back_sems)
    unpack_rows(back[2])

    def unpack(which):
        for p in range(2):
            for half in range(2):
                turned[which * 2 + half, pl.ds(p, devices, stride=2), :] = rows_f32[pl.ds(which * 4 + p * 2 + half, devices, stride=8), :]
        return jnp.concatenate([turned[which * 2], turned[which * 2 + 1]], 1)

    x_res[...] = jnp.transpose(unpack(0)).astype(kind)
    y_res[...] = unpack(1).astype(kind)


def final_kernel(states, data, res_z, res_x, res_y, out):
    w = [states[k] for k in range(4)]
    z = [2.0 * data[...] - w[0]]
    z += [w[k + 1] - 2.0 * res[...].astype(jnp.float32) for k, res in enumerate((res_z, res_x, res_y))]
    twice = 0.5 * (z[0] + z[1] + z[2] + z[3])
    for k in range(4):
        out[k] = (1.0 - relaxation) * w[k] + relaxation * (twice - z[k])


def fourier_tables(length):
    indices = np.arange(length, dtype=np.int32)
    phase = indices[:, None] * indices[None, :] % length
    angle = phase.astype(np.float32) * np.float32(2.0 * math.pi / length)
    return (jnp.asarray(np.cos(angle), jnp.bfloat16), jnp.asarray(np.sin(angle), jnp.bfloat16))


def constants(width):
    kind = jnp.bfloat16
    tables = (first_table(), last_table(), spread_table(width), gather_table(width))
    return tuple(jnp.asarray(table.astype(kind)) for table in tables)


def on_device(states, measured, response, kernel_in, bias_in, kernel_mid, bias_mid, kernel_out):
    current = states[:, 0, 0]
    width = current.shape[-1]
    depth = lax.axis_size("plane")
    kind = jnp.bfloat16
    args = (current, measured[0, 0], response) + fourier_tables(width)
    args += (jnp.transpose(kernel_in, (0, 1, 3, 2)), bias_in, kernel_mid, bias_mid, jnp.transpose(kernel_out, (1, 0, 2))) + constants(width)
    short = pltpu.VMEM((width, width), kind)
    image = pltpu.VMEM((width, width), jnp.float32)
    by_core = pltpu.VMEM((2, depth, 8, 128), kind)
    by_chip = pltpu.VMEM((depth, 2, 8, 128), kind)
    sharp = jax.ShapeDtypeStruct((width, width), jnp.float32)
    coarse = jax.ShapeDtypeStruct((width, width), kind)
    found = pl.pallas_call(
        functools.partial(whole_kernel, depth),
        out_shape=(sharp, coarse, coarse, coarse),
        in_specs=[pl.BlockSpec(memory_space=pl.ANY)] * 5 + [pl.BlockSpec(memory_space=pltpu.VMEM)] * (len(args) - 5),
        out_specs=(pl.BlockSpec(memory_space=pltpu.VMEM),) * 4,
        scratch_shapes=built_shapes(1) + built_shapes(2) + built_shapes(2)
        + work_shapes(1, 1, width) + work_shapes(2, 2, depth)
        + [short, short, pltpu.VMEM((4, width, 128), jnp.float32), pltpu.VMEM((2 * depth * 8, 128), jnp.float32)]
        + [by_core, by_chip, by_chip] * 2
        + [pltpu.VMEM((4, width, width), jnp.float32), image, image, short, short, pltpu.SemaphoreType.DMA((8,))]
        + [pltpu.SemaphoreType.DMA] * 12,
        compiler_params=pltpu.CompilerParams(vmem_limit_bytes=60 * 2**20, collective_id=0, has_side_effects=True),
        cost_estimate=pl.CostEstimate(flops=12 * 10**9, bytes_accessed=2**22, transcendentals=0),
    )(*args)
    step = width // 2
    flat = pl.BlockSpec((step, width), lambda i: (i, 0))
    deep = pl.BlockSpec((4, step, width), lambda i: (0, i, 0))
    out = pl.pallas_call(
        final_kernel,
        grid=(2,),
        out_shape=jax.ShapeDtypeStruct(current.shape, jnp.float32),
        in_specs=[deep, flat, flat, flat, flat],
        out_specs=deep,
        cost_estimate=pl.CostEstimate(flops=2 * 10**6, bytes_accessed=2**21, transcendentals=0),
    )(current, *found)
    return out[:, None, None]


def solution(mesh):
    placed = (
        P(None, "frame", "plane", None, None),
        P("frame", "plane", None, None),
        P(),
        P(),
        P(),
        P(),
        P(),
        P(),
    )
    return jax.shard_map(
        on_device,
        mesh=mesh,
        in_specs=placed,
        out_specs=P(None, "frame", "plane", None, None),
        check_vma=False,
    )
```

```python
import functools
import math

import jax
import jax.numpy as jnp
import numpy as np
from jax import lax
from jax.experimental import pallas as pl
from jax.experimental.pallas import tpu as pltpu
from jax.sharding import PartitionSpec as P

relaxation = 0.8
MESH = pl.DeviceIdType.MESH
UNROLL = 8

GROUPS = [(0, 0), (0, 1), (3, 0), (3, 1), (1, 0), (1, 1), (2, 0), (2, 1)]
STRIP = 16
FIRST_STEP = 8
MID_STEP = 16


def block_order(width):
    blocks = width // 2
    per = blocks // STRIP
    lane = np.arange(blocks)
    return (lane % STRIP) * per + lane // STRIP


def spread_table(width):
    blocks = width // 2
    order = block_order(width)
    table = np.zeros((width, 4 * blocks), np.float32)
    for xo in range(4):
        for lane in range(blocks):
            col = 2 * order[lane] + xo - 1
            if 0 <= col < width:
                table[col, xo * blocks + lane] = 1
    return table


def gather_table(width):
    blocks = width // 2
    order = block_order(width)
    table = np.zeros((width, width), np.float32)
    for j in range(2):
        for lane in range(blocks):
            table[j * blocks + lane, 2 * order[lane] + j] = 1
    return table


def select_in():
    chosen = np.zeros((9, 4, 24, 2, 8), np.float32)
    for half in range(2):
        for g, (i, j) in enumerate(GROUPS):
            for p in range(3):
                for q in range(3):
                    chosen[3 * p + q, j + q, 7 + 4 * half + i + p, half, g] = 1
    return chosen.reshape(9, 96, 16)


def slots_mid():
    slots = list(GROUPS)
    slots += [(i, -1 if j == 1 else 2) for i, j in GROUPS]
    slots += [(-1 if i == 3 else 4, j) for i, j in GROUPS[:4]]
    slots += [(-1 if i == 3 else 4, -1 if j == 1 else 2) for i, j in GROUPS[:4]]
    return slots


def select_mid():
    chosen = np.zeros((9, 24, 8), np.float32)
    for s, (row, col) in enumerate(slots_mid()):
        for g, (i, j) in enumerate(GROUPS):
            p, q = row - i + 1, col - j + 1
            if 0 <= p < 3 and 0 <= q < 3:
                chosen[3 * p + q, s, g] = 1
    return chosen


def select_out():
    targets = [None] * 32
    for j in range(2):
        far = 2 if j == 0 else -1
        for i in range(4):
            targets[j * 4 + i] = (i, j)
            targets[8 + j * 4 + i] = (i, far)
        for base, col in ((16, j), (24, far)):
            targets[base + j * 4] = (4, col)
            targets[base + j * 4 + 3] = (-1, col)
    chosen = np.zeros((9, 32, 8), np.float32)
    for r, target in enumerate(targets):
        if target is None:
            continue
        for g, (i, j) in enumerate(GROUPS):
            p, q = i - target[0] + 1, j - target[1] + 1
            if 0 <= p < 3 and 0 <= q < 3:
                chosen[3 * p + q, r, g] = 1
    return chosen


def first_table():
    chosen = select_in()
    table = np.zeros((2, 96, 16, 32), np.float32)
    for ch in range(2):
        for tap in range(9):
            table[ch, :, :, 2 * tap + ch] = chosen[tap]
    return table.reshape(192, 512)


def last_table():
    table = np.zeros((32, 8, 16), np.float32)
    table[:, :, :9] = select_out().transpose(1, 2, 0)
    return table.reshape(32, 128)


def mm(a, b, dims=((1,), (0,))):
    return lax.dot_general(a, b, (dims, ((), ())), preferred_element_type=jnp.float32)


def prepare(d, params, tables, built, frames):
    kernel_in, bias_in, kernel_mid, bias_mid, kernel_out = params
    first_at, last_at = tables
    w_first, b_first, w_mid, b_mid, w_last, spare = built
    kind = jnp.bfloat16
    lane = lax.broadcasted_iota(jnp.int32, (32, 512), 1)
    row = lax.broadcasted_iota(jnp.int32, (32, 512), 0)
    repeat = (lane % 32 == row).astype(jnp.float32)
    wide = repeat.astype(kind)
    narrow = wide[:, :256]

    spare[...] = jnp.zeros_like(spare)
    for tap in range(9):
        spare[2 * tap:2 * tap + 2, :] = mm(kernel_in[d, tap], wide)
    tiled = jnp.concatenate([spare[...]] * 16, 0)
    own = lax.broadcasted_iota(jnp.int32, (512, 512), 0) // 32 == lax.broadcasted_iota(jnp.int32, (512, 512), 1) // 32
    built_first = mm(first_at[...], jnp.where(own, tiled, 0.0).astype(kind)).astype(kind)
    w_first[:, 0:512] = built_first
    exact = lax.dot_general(bias_in[...], repeat, (((1,), (0,)), ((), ())), precision=lax.Precision.HIGHEST, preferred_element_type=jnp.float32)
    b_first[0:1, 0:512] = exact[d:d + 1]
    if frames == 2:
        w_first[0:96, 512:1024] = built_first[96:192]
        w_first[96:192, 512:1024] = built_first[0:96]
        b_first[0:1, 512:1024] = exact[d:d + 1]
    exact = lax.dot_general(bias_mid[:, 0, :], repeat[:, :256], (((1,), (0,)), ((), ())), precision=lax.Precision.HIGHEST, preferred_element_type=jnp.float32)
    b_mid[0:1, :] = exact[d:d + 1]

    taps = [mm(kernel_mid[d, 0, tap], narrow, ((0,), (0,))) for tap in range(9)]
    group = lane[:, :256] // 32
    for s, (r, c) in enumerate(slots_mid()):
        value = jnp.zeros((32, 256), jnp.float32)
        for g, (i, j) in enumerate(GROUPS):
            p, q = r - i + 1, c - j + 1
            if 0 <= p < 3 and 0 <= q < 3:
                value = jnp.where(group == g, taps[3 * p + q], value)
        w_mid[s * 32:(s + 1) * 32, :] = value.astype(kind)

    spare[9:16, 0:256] = jnp.zeros((7, 256), jnp.float32)
    spare[0:9, 0:256] = mm(kernel_out[:, d, :], narrow)
    tiled = jnp.concatenate([spare[0:16, 0:256]] * 8, 0)
    own = lax.broadcasted_iota(jnp.int32, (128, 256), 0) // 16 == lax.broadcasted_iota(jnp.int32, (128, 256), 1) // 32
    w_last[...] = mm(last_at[...], jnp.where(own, tiled, 0.0).astype(kind)).astype(kind)


def first_half(x, built, spread, u_ref, h_ref, c_ref, frames):
    w_first, b_first = built[:2]
    rows = u_ref.shape[1] - 16
    row_blocks = rows // 4
    images = len(x) * frames
    kind = jnp.bfloat16
    for pair in range(len(x)):
        for ch in range(2):
            u_ref[pair * 2 + ch, :8, :] = jnp.zeros((8, 512), jnp.float32)
            u_ref[pair * 2 + ch, rows + 8:, :] = jnp.zeros((8, 512), jnp.float32)
            u_ref[pair * 2 + ch, 8:rows + 8, :] = mm(x[pair][ch](), spread)
    for img in range(images):
        h_ref[img, 0] = jnp.zeros((160, 256), kind)
        h_ref[img, row_blocks + 1] = jnp.zeros((160, 256), kind)
        c_ref[img, 0] = jnp.zeros((32, 128), jnp.float32)
        c_ref[img, row_blocks + 1] = jnp.zeros((32, 128), jnp.float32)

    strip = lax.broadcasted_iota(jnp.int32, (16, 256), 0)
    first_strip = strip == 0
    last_strip = strip == 15

    def first_layer(step, carry):
        for pair in range(len(x)):
            parts = []
            for ch in range(2):
                for xo in range(4):
                    parts.append(jnp.concatenate([
                        u_ref[pair * 2 + ch, pl.ds(pl.multiple_of((step * FIRST_STEP + k) * 8, 8), 24), xo * 128:(xo + 1) * 128]
                        for k in range(FIRST_STEP)], 1))
            stacked = jnp.concatenate(parts, 0).astype(kind)
            made = mm(stacked, w_first[...], ((0,), (0,)))
            made = jnp.maximum(made + b_first[0:1, :], 0.0)
            for f in range(frames):
                for k in range(FIRST_STEP):
                    for half in range(2):
                        at = f * 512 + half * 256
                        piece = made[k * 128:(k + 1) * 128, at:at + 256]
                        to = h_ref.at[pair * frames + f, 2 * (step * FIRST_STEP + k) + half + 1]
                        to[16:144, :] = piece.astype(kind)
                        to[0:16, :] = jnp.where(first_strip, 0.0, pltpu.roll(piece[112:128], 1, 0)).astype(kind)
                        to[144:160, :] = jnp.where(last_strip, 0.0, pltpu.roll(piece[0:16], 15, 0)).astype(kind)
        return carry

    lax.fori_loop(0, rows // 8 // FIRST_STEP, first_layer, 0)


def second_half(built, gather, emit, h_ref, c_ref, frames):
    w_mid, b_mid, w_last = built[2:5]
    images = h_ref.shape[0]
    row_blocks = h_ref.shape[1] - 2
    rows = row_blocks * 4
    kind = jnp.bfloat16
    n = MID_STEP * 128
    right = (lax.broadcasted_iota(jnp.int32, (n, 256), 1) // 32) % 2 == 1
    right_half = right[:, :128]
    low = lax.broadcasted_iota(jnp.int32, (n, 128), 1) >= 64
    steps = row_blocks // MID_STEP

    def mid_layer(at, carry):
        img, a = at // steps, (at % steps) * MID_STEP

        def part(down, shift, lanes):
            return h_ref[img, pl.ds(a + 1 + down, MID_STEP), 16 + shift:144 + shift, 0:lanes].reshape(n, lanes)

        here = part(0, 0, 256)
        side = jnp.where(right, part(0, -16, 256), part(0, 16, 256))
        across = jnp.where(low, part(-1, 0, 128), part(1, 0, 128))
        corner_left = jnp.where(low, part(-1, -16, 128), part(1, -16, 128))
        corner_right = jnp.where(low, part(-1, 16, 128), part(1, 16, 128))
        corner = jnp.where(right_half, corner_left, corner_right)
        made = mm(jnp.concatenate([here, side, across, corner], 1), w_mid[...])
        hidden = jnp.maximum(made + b_mid[0:1, :], 0.0).astype(kind)
        last = mm(w_last[...], hidden, ((1,), (1,)))
        for k in range(MID_STEP):
            c_ref[img, a + 1 + k] = last[:, k * 128:(k + 1) * 128]
        return carry

    lax.fori_loop(0, images * steps, mid_layer, 0)

    lane = lax.broadcasted_iota(jnp.int32, (row_blocks * 8, 128), 1)
    sub = lax.broadcasted_iota(jnp.int32, (row_blocks * 8, 128), 0) % 8
    half_sub = sub[:row_blocks * 4]

    def moved(value):
        before = jnp.where(lane >= 16, pltpu.roll(value, 16, 1), jnp.where(lane >= 1, pltpu.roll(value, 17, 1), 0.0))
        after = jnp.where(lane < 112, pltpu.roll(value, 112, 1), jnp.where(lane < 127, pltpu.roll(value, 111, 1), 0.0))
        return jnp.where(sub < 4, before, after)

    for img in range(images):

        def piece(at, down=0):
            return c_ref[img, 1 + down:1 + down + row_blocks, at:at + 8, :].reshape(row_blocks * 8, 128)

        total = piece(0) + moved(piece(8))
        edges = piece(16) + moved(piece(24))
        c_ref[img, 1:1 + row_blocks, 16:24, :] = edges.reshape(row_blocks, 8, 128)
        total += jnp.where(sub % 4 == 0, piece(16, -1), 0.0) + jnp.where(sub % 4 == 3, piece(16, 1), 0.0)
        twos = total.reshape(row_blocks // 2, 16, 128)
        even = twos[:, 0:8].reshape(row_blocks * 4, 128)
        odd = twos[:, 8:16].reshape(row_blocks * 4, 128)
        left = jnp.where(half_sub < 4, even, pltpu.roll(odd, 4, 0))
        right_side = jnp.where(half_sub < 4, pltpu.roll(even, rows - 4, 0), odd)
        emit(img // frames, img % frames, mm(jnp.concatenate([left, right_side], 1).astype(kind), gather))


def built_shapes(frames):
    return [
        pltpu.VMEM((192, frames * 512), jnp.bfloat16),
        pltpu.VMEM((8, frames * 512), jnp.float32),
        pltpu.VMEM((768, 256), jnp.bfloat16),
        pltpu.VMEM((8, 256), jnp.float32),
        pltpu.VMEM((32, 256), jnp.bfloat16),
        pltpu.VMEM((32, 512), jnp.float32),
    ]


def work_shapes(pairs, frames, rows):
    images = pairs * frames
    return [
        pltpu.VMEM((pairs * 2, rows + 16, 512), jnp.float32),
        pltpu.VMEM((images, rows // 4 + 2, 160, 256), jnp.bfloat16),
        pltpu.VMEM((images, rows // 4 + 2, 32, 128), jnp.float32),
    ]


def filtered(source, response, cos, sin):
    kind = jnp.bfloat16
    row_real = mm(source, cos).astype(kind)
    row_imag = (-mm(source, sin)).astype(kind)
    gain = 1.0 / (1.0 + response)
    spec_real = ((mm(cos, row_real) + mm(sin, row_imag)) * gain).astype(kind)
    spec_imag = ((mm(cos, row_imag) - mm(sin, row_real)) * gain).astype(kind)
    back_real = (mm(cos, spec_real) - mm(sin, spec_imag)).astype(kind)
    back_imag = (mm(cos, spec_imag) + mm(sin, spec_real)).astype(kind)
    return (mm(back_real, cos) - mm(back_imag, sin)) * (1.0 / (source.shape[0] * source.shape[1]))


def whole_kernel(depth, states_at, measured_at, response_at, cosine_at, sines_at, *rest):
    params, first_at, last_at, spread_at, gather_at = rest[:5], rest[5], rest[6], rest[7], rest[8]
    data, z_res, x_res, y_res = rest[9:13]
    rest = rest[13:]
    built = [rest[0:6], rest[6:12], rest[12:18]]
    z_work, xy_work = rest[18:21], rest[21:24]
    z_own, z_other, turned, rows_f32 = rest[24:28]
    there, back = rest[28:31], rest[31:34]
    states, measured, response, cosine, sines, loaded = rest[34:40]
    z_send, z_recv = rest[40:42]
    there_sems, back_sems = rest[42:47], rest[47:52]
    first, spread, gather = rest[52:]
    tables = first, last_at
    kind = jnp.bfloat16
    devices = 2 * depth
    frame = lax.axis_index("frame")
    plane = lax.axis_index("plane")
    chips = devices // 2
    chip = (frame * depth + plane) // 2
    core = (frame * depth + plane) % 2
    sibling = (frame, plane + 1 - 2 * core)

    def at(k):
        other = (chip ^ k) * 2 + core
        return chip ^ k, (other // depth, other % depth)

    barrier = pltpu.get_barrier_semaphore()

    def greet(k, carry):
        pl.semaphore_signal(barrier, inc=1, device_id=at(k)[1], device_id_type=MESH)
        return carry

    loads = [pltpu.make_async_copy(states_at.at[k], states.at[k], loaded.at[k]) for k in range(4)]
    for k, (source, target) in enumerate(((measured_at, measured), (response_at, response), (cosine_at, cosine), (sines_at, sines))):
        loads.append(pltpu.make_async_copy(source, target, loaded.at[4 + k]))
    for k, (source, target) in enumerate(((first_at, first), (spread_at, spread), (gather_at, gather))):
        loads.append(pltpu.make_async_copy(source, target, loaded.at[8 + k]))
    for k in (2, 3, 1, 8, 0, 4, 5, 6, 7, 9, 10):
        loads[k].start()
    pl.semaphore_signal(barrier, inc=1, device_id=sibling, device_id_type=MESH)
    lax.fori_loop(1, chips, greet, 0, unroll=UNROLL)

    def pack(buffer):
        value = rows_f32[...].astype(kind).reshape(chips, 2, 8, 128)
        buffer[0] = value[:, 0]
        buffer[1] = value[:, 1]

    def unpack_rows(buffer):
        rows_f32[...] = buffer[...].astype(jnp.float32).reshape(devices * 8, 128)

    def within_chip(buffers, sems):
        source, mixed, _ = buffers
        keep, send, recv, _, _ = sems
        moves = [
            pltpu.make_async_copy(source.at[core], mixed.at[:, core], keep),
            pltpu.make_async_remote_copy(
                src_ref=source.at[1 - core], dst_ref=mixed.at[:, core], send_sem=send, recv_sem=recv,
                device_id=sibling, device_id_type=MESH,
            ),
        ]
        for move in moves:
            move.start()
        return moves

    loads[2].wait()
    loads[3].wait()
    for which, value in enumerate((jnp.transpose(states[2]), states[3])):
        for half in range(2):
            turned[which * 2 + half] = value[:, half * 128:(half + 1) * 128]
        for p in range(2):
            for half in range(2):
                rows_f32[pl.ds(which * 4 + p * 2 + half, devices, stride=8), :] = turned[which * 2 + half, pl.ds(p, devices, stride=2), :]
    pack(there[0])
    loads[1].wait()
    z_own[...] = states[1].astype(kind)
    pl.semaphore_wait(barrier, chips)

    def between_chips(buffers, sems, moves):
        _, mixed, target = buffers
        _, _, _, send, recv = sems
        for move in moves:
            move.wait()
        pltpu.make_async_copy(mixed.at[chip], target.at[chip], recv).start()

        def go(k, carry):
            other, coordinates = at(k)
            pltpu.make_async_remote_copy(
                src_ref=mixed.at[other], dst_ref=target.at[chip], send_sem=send, recv_sem=recv,
                device_id=coordinates, device_id_type=MESH,
            ).start()
            return carry

        lax.fori_loop(1, chips, go, 0, unroll=UNROLL)

    def finish(buffers, sems):
        _, mixed, target = buffers
        pltpu.make_async_copy(target, target, sems[4]).wait()
        some = mixed.at[pl.ds(0, chips - 1)]
        pltpu.make_async_copy(some, some, sems[3]).wait()

    there_moves = within_chip(there, there_sems)
    swap = pltpu.make_async_remote_copy(
        src_ref=z_own, dst_ref=z_other, send_sem=z_send, recv_sem=z_recv,
        device_id=(1 - frame, plane), device_id_type=MESH,
    )
    loads[8].wait()
    prepare(0, params, tables, built[0], 1)
    prepare(1, params, tables, built[1], 2)
    between_chips(there, there_sems, there_moves)
    swap.start()
    prepare(2, params, tables, built[2], 2)
    for k in (0, 4, 5, 6, 7, 9, 10):
        loads[k].wait()
    source = (measured[...] + states[0]).astype(kind)
    data[...] = filtered(source, response[...], cosine[...], sines[...])

    finish(there, there_sems)
    unpack_rows(there[2])

    def rows_of(which, p, f, half):
        return pl.ds(f * depth * 8 + which * 4 + p * 2 + half, depth, stride=8)

    for which in range(2):

        def plane_of(p, f):
            return jnp.concatenate([rows_f32[rows_of(which, p, f, half), :] for half in range(2)], 1).astype(kind)

        def emit(p, f, value):
            for half in range(2):
                rows_f32[rows_of(which, p, f, half), :] = value[:, half * 128:(half + 1) * 128]

        pairs = [(functools.partial(plane_of, p, 0), functools.partial(plane_of, p, 1)) for p in range(2)]
        first_half(pairs, built[which + 1], spread[...], *xy_work, frames=2)
        second_half(built[which + 1], gather[...], emit, *xy_work[1:], frames=2)
    pack(back[0])
    back_moves = within_chip(back, back_sems)

    def emit_z(p, f, value):
        z_res[...] = value.astype(kind)

    swap.wait()
    first_half([(lambda: z_own[...], lambda: z_other[...])], built[0], spread[...], *z_work, frames=1)
    between_chips(back, back_sems, back_moves)
    second_half(built[0], gather[...], emit_z, *z_work[1:], frames=1)
    finish(back, back_sems)
    unpack_rows(back[2])

    def unpack(which):
        for p in range(2):
            for half in range(2):
                turned[which * 2 + half, pl.ds(p, devices, stride=2), :] = rows_f32[pl.ds(which * 4 + p * 2 + half, devices, stride=8), :]
        return jnp.concatenate([turned[which * 2], turned[which * 2 + 1]], 1)

    x_res[...] = jnp.transpose(unpack(0)).astype(kind)
    y_res[...] = unpack(1).astype(kind)


def final_kernel(states, data, res_z, res_x, res_y, out):
    w = [states[k] for k in range(4)]
    z = [2.0 * data[...] - w[0]]
    z += [w[k + 1] - 2.0 * res[...].astype(jnp.float32) for k, res in enumerate((res_z, res_x, res_y))]
    twice = 0.5 * (z[0] + z[1] + z[2] + z[3])
    for k in range(4):
        out[k] = (1.0 - relaxation) * w[k] + relaxation * (twice - z[k])


def fourier_tables(length):
    indices = np.arange(length, dtype=np.int32)
    phase = indices[:, None] * indices[None, :] % length
    angle = phase.astype(np.float32) * np.float32(2.0 * math.pi / length)
    return (jnp.asarray(np.cos(angle), jnp.bfloat16), jnp.asarray(np.sin(angle), jnp.bfloat16))


def constants(width):
    kind = jnp.bfloat16
    tables = (first_table(), last_table(), spread_table(width), gather_table(width))
    return tuple(jnp.asarray(table.astype(kind)) for table in tables)


def on_device(states, measured, response, kernel_in, bias_in, kernel_mid, bias_mid, kernel_out):
    current = states[:, 0, 0]
    width = current.shape[-1]
    depth = lax.axis_size("plane")
    kind = jnp.bfloat16
    args = (current, measured[0, 0], response) + fourier_tables(width)
    args += (jnp.transpose(kernel_in, (0, 1, 3, 2)), bias_in, kernel_mid, bias_mid, jnp.transpose(kernel_out, (1, 0, 2))) + constants(width)
    short = pltpu.VMEM((width, width), kind)
    image = pltpu.VMEM((width, width), jnp.float32)
    by_core = pltpu.VMEM((2, depth, 8, 128), kind)
    by_chip = pltpu.VMEM((depth, 2, 8, 128), kind)
    sharp = jax.ShapeDtypeStruct((width, width), jnp.float32)
    coarse = jax.ShapeDtypeStruct((width, width), kind)
    found = pl.pallas_call(
        functools.partial(whole_kernel, depth),
        out_shape=(sharp, coarse, coarse, coarse),
        in_specs=[pl.BlockSpec(memory_space=pltpu.VMEM if 5 <= k < 10 or k == 11 else pl.ANY) for k in range(len(args))],
        out_specs=(pl.BlockSpec(memory_space=pltpu.VMEM),) * 4,
        scratch_shapes=built_shapes(1) + built_shapes(2) + built_shapes(2)
        + work_shapes(1, 1, width) + work_shapes(2, 2, depth)
        + [short, short, pltpu.VMEM((4, width, 128), jnp.float32), pltpu.VMEM((2 * depth * 8, 128), jnp.float32)]
        + [by_core, by_chip, by_chip] * 2
        + [pltpu.VMEM((4, width, width), jnp.float32), image, image, short, short, pltpu.SemaphoreType.DMA((11,))]
        + [pltpu.SemaphoreType.DMA] * 12
        + [pltpu.VMEM(table.shape, kind) for table in (args[10], args[12], args[13])],
        compiler_params=pltpu.CompilerParams(vmem_limit_bytes=60 * 2**20, collective_id=0, has_side_effects=True),
        cost_estimate=pl.CostEstimate(flops=12 * 10**9, bytes_accessed=2**22, transcendentals=0),
    )(*args)
    step = width // 2
    flat = pl.BlockSpec((step, width), lambda i: (i, 0))
    deep = pl.BlockSpec((4, step, width), lambda i: (0, i, 0))
    out = pl.pallas_call(
        final_kernel,
        grid=(2,),
        out_shape=jax.ShapeDtypeStruct(current.shape, jnp.float32),
        in_specs=[deep, flat, flat, flat, flat],
        out_specs=deep,
        cost_estimate=pl.CostEstimate(flops=2 * 10**6, bytes_accessed=2**21, transcendentals=0),
    )(current, *found)
    return out[:, None, None]


def solution(mesh):
    placed = (
        P(None, "frame", "plane", None, None),
        P("frame", "plane", None, None),
        P(),
        P(),
        P(),
        P(),
        P(),
        P(),
    )
    return jax.shard_map(
        on_device,
        mesh=mesh,
        in_specs=placed,
        out_specs=P(None, "frame", "plane", None, None),
        check_vma=False,
    )
```

```python
import functools
import math

import jax
import jax.numpy as jnp
import numpy as np
from jax import lax
from jax.experimental import pallas as pl
from jax.experimental.pallas import tpu as pltpu
from jax.sharding import PartitionSpec as P

relaxation = 0.8
MESH = pl.DeviceIdType.MESH
UNROLL = 8

GROUPS = [(0, 0), (0, 1), (3, 0), (3, 1), (1, 0), (1, 1), (2, 0), (2, 1)]
STRIP = 16
FIRST_STEP = 8
MID_STEP = 16


def block_order(width):
    blocks = width // 2
    per = blocks // STRIP
    lane = np.arange(blocks)
    return (lane % STRIP) * per + lane // STRIP


def spread_table(width):
    blocks = width // 2
    order = block_order(width)
    table = np.zeros((width, 4 * blocks), np.float32)
    for xo in range(4):
        for lane in range(blocks):
            col = 2 * order[lane] + xo - 1
            if 0 <= col < width:
                table[col, xo * blocks + lane] = 1
    return table


def gather_table(width):
    blocks = width // 2
    order = block_order(width)
    table = np.zeros((width, width), np.float32)
    for j in range(2):
        for lane in range(blocks):
            table[j * blocks + lane, 2 * order[lane] + j] = 1
    return table


def select_in():
    chosen = np.zeros((9, 4, 24, 2, 8), np.float32)
    for half in range(2):
        for g, (i, j) in enumerate(GROUPS):
            for p in range(3):
                for q in range(3):
                    chosen[3 * p + q, j + q, 7 + 4 * half + i + p, half, g] = 1
    return chosen.reshape(9, 96, 16)


def slots_mid():
    slots = list(GROUPS)
    slots += [(i, -1 if j == 1 else 2) for i, j in GROUPS]
    slots += [(-1 if i == 3 else 4, j) for i, j in GROUPS[:4]]
    slots += [(-1 if i == 3 else 4, -1 if j == 1 else 2) for i, j in GROUPS[:4]]
    return slots


def select_mid():
    chosen = np.zeros((9, 24, 8), np.float32)
    for s, (row, col) in enumerate(slots_mid()):
        for g, (i, j) in enumerate(GROUPS):
            p, q = row - i + 1, col - j + 1
            if 0 <= p < 3 and 0 <= q < 3:
                chosen[3 * p + q, s, g] = 1
    return chosen


def select_out():
    targets = [None] * 32
    for j in range(2):
        far = 2 if j == 0 else -1
        for i in range(4):
            targets[j * 4 + i] = (i, j)
            targets[8 + j * 4 + i] = (i, far)
        for base, col in ((16, j), (24, far)):
            targets[base + j * 4] = (4, col)
            targets[base + j * 4 + 3] = (-1, col)
    chosen = np.zeros((9, 32, 8), np.float32)
    for r, target in enumerate(targets):
        if target is None:
            continue
        for g, (i, j) in enumerate(GROUPS):
            p, q = i - target[0] + 1, j - target[1] + 1
            if 0 <= p < 3 and 0 <= q < 3:
                chosen[3 * p + q, r, g] = 1
    return chosen


def first_table():
    chosen = select_in()
    table = np.zeros((2, 96, 16, 32), np.float32)
    for ch in range(2):
        for tap in range(9):
            table[ch, :, :, 2 * tap + ch] = chosen[tap]
    return table.reshape(192, 512)


def last_table():
    table = np.zeros((32, 8, 16), np.float32)
    table[:, :, :9] = select_out().transpose(1, 2, 0)
    return table.reshape(32, 128)


def mm(a, b, dims=((1,), (0,))):
    return lax.dot_general(a, b, (dims, ((), ())), preferred_element_type=jnp.float32)


def prepare(d, params, tables, built, frames):
    kernel_in, bias_in, kernel_mid, bias_mid, kernel_out = params
    first_at, last_at = tables
    w_first, b_first, w_mid, b_mid, w_last, spare = built
    kind = jnp.bfloat16
    lane = lax.broadcasted_iota(jnp.int32, (32, 512), 1)
    row = lax.broadcasted_iota(jnp.int32, (32, 512), 0)
    repeat = (lane % 32 == row).astype(jnp.float32)
    wide = repeat.astype(kind)
    narrow = wide[:, :256]

    spare[...] = jnp.zeros_like(spare)
    for tap in range(9):
        spare[2 * tap:2 * tap + 2, :] = mm(kernel_in[d, tap], wide)
    tiled = jnp.concatenate([spare[...]] * 16, 0)
    own = lax.broadcasted_iota(jnp.int32, (512, 512), 0) // 32 == lax.broadcasted_iota(jnp.int32, (512, 512), 1) // 32
    built_first = mm(first_at[...], jnp.where(own, tiled, 0.0).astype(kind)).astype(kind)
    w_first[:, 0:512] = built_first
    exact = lax.dot_general(bias_in[...], repeat, (((1,), (0,)), ((), ())), precision=lax.Precision.HIGHEST, preferred_element_type=jnp.float32)
    b_first[0:1, 0:512] = exact[d:d + 1]
    if frames == 2:
        w_first[0:96, 512:1024] = built_first[96:192]
        w_first[96:192, 512:1024] = built_first[0:96]
        b_first[0:1, 512:1024] = exact[d:d + 1]
    exact = lax.dot_general(bias_mid[:, 0, :], repeat[:, :256], (((1,), (0,)), ((), ())), precision=lax.Precision.HIGHEST, preferred_element_type=jnp.float32)
    b_mid[0:1, :] = exact[d:d + 1]

    taps = [mm(kernel_mid[d, 0, tap], narrow, ((0,), (0,))) for tap in range(9)]
    group = lane[:, :256] // 32
    for s, (r, c) in enumerate(slots_mid()):
        value = jnp.zeros((32, 256), jnp.float32)
        for g, (i, j) in enumerate(GROUPS):
            p, q = r - i + 1, c - j + 1
            if 0 <= p < 3 and 0 <= q < 3:
                value = jnp.where(group == g, taps[3 * p + q], value)
        w_mid[s * 32:(s + 1) * 32, :] = value.astype(kind)

    spare[9:16, 0:256] = jnp.zeros((7, 256), jnp.float32)
    spare[0:9, 0:256] = mm(kernel_out[:, d, :], narrow)
    tiled = jnp.concatenate([spare[0:16, 0:256]] * 8, 0)
    own = lax.broadcasted_iota(jnp.int32, (128, 256), 0) // 16 == lax.broadcasted_iota(jnp.int32, (128, 256), 1) // 32
    w_last[...] = mm(last_at[...], jnp.where(own, tiled, 0.0).astype(kind)).astype(kind)


def first_half(x, built, spread, u_ref, h_ref, c_ref, frames):
    w_first, b_first = built[:2]
    rows = u_ref.shape[1] - 16
    row_blocks = rows // 4
    images = len(x) * frames
    kind = jnp.bfloat16
    for pair in range(len(x)):
        for ch in range(2):
            u_ref[pair * 2 + ch, :8, :] = jnp.zeros((8, 512), jnp.float32)
            u_ref[pair * 2 + ch, rows + 8:, :] = jnp.zeros((8, 512), jnp.float32)
            u_ref[pair * 2 + ch, 8:rows + 8, :] = mm(x[pair][ch](), spread)
    for img in range(images):
        h_ref[img, 0] = jnp.zeros((160, 256), kind)
        h_ref[img, row_blocks + 1] = jnp.zeros((160, 256), kind)
        c_ref[img, 0] = jnp.zeros((32, 128), jnp.float32)
        c_ref[img, row_blocks + 1] = jnp.zeros((32, 128), jnp.float32)

    strip = lax.broadcasted_iota(jnp.int32, (16, 256), 0)
    first_strip = strip == 0
    last_strip = strip == 15

    def first_layer(step, carry):
        for pair in range(len(x)):
            parts = []
            for ch in range(2):
                for xo in range(4):
                    parts.append(jnp.concatenate([
                        u_ref[pair * 2 + ch, pl.ds(pl.multiple_of((step * FIRST_STEP + k) * 8, 8), 24), xo * 128:(xo + 1) * 128]
                        for k in range(FIRST_STEP)], 1))
            stacked = jnp.concatenate(parts, 0).astype(kind)
            made = mm(stacked, w_first[...], ((0,), (0,)))
            made = jnp.maximum(made + b_first[0:1, :], 0.0)
            for f in range(frames):
                for k in range(FIRST_STEP):
                    for half in range(2):
                        at = f * 512 + half * 256
                        piece = made[k * 128:(k + 1) * 128, at:at + 256]
                        to = h_ref.at[pair * frames + f, 2 * (step * FIRST_STEP + k) + half + 1]
                        to[16:144, :] = piece.astype(kind)
                        to[0:16, :] = jnp.where(first_strip, 0.0, pltpu.roll(piece[112:128], 1, 0)).astype(kind)
                        to[144:160, :] = jnp.where(last_strip, 0.0, pltpu.roll(piece[0:16], 15, 0)).astype(kind)
        return carry

    lax.fori_loop(0, rows // 8 // FIRST_STEP, first_layer, 0)


def second_half(built, gather, emit, h_ref, c_ref, frames, between=None):
    w_mid, b_mid, w_last = built[2:5]
    images = h_ref.shape[0]
    row_blocks = h_ref.shape[1] - 2
    rows = row_blocks * 4
    kind = jnp.bfloat16
    together = min(2, images)
    n = together * MID_STEP * 128
    right = (lax.broadcasted_iota(jnp.int32, (n, 256), 1) // 32) % 2 == 1
    right_half = right[:, :128]
    low = lax.broadcasted_iota(jnp.int32, (n, 128), 1) >= 64
    steps = row_blocks // MID_STEP

    def mid_layer(at, carry):
        img, a = at // steps * together, (at % steps) * MID_STEP

        def part(down, shift, lanes):
            return h_ref[pl.ds(img, together), pl.ds(a + 1 + down, MID_STEP), 16 + shift:144 + shift, 0:lanes].reshape(n, lanes)

        here = part(0, 0, 256)
        side = jnp.where(right, part(0, -16, 256), part(0, 16, 256))
        across = jnp.where(low, part(-1, 0, 128), part(1, 0, 128))
        corner_left = jnp.where(low, part(-1, -16, 128), part(1, -16, 128))
        corner_right = jnp.where(low, part(-1, 16, 128), part(1, 16, 128))
        corner = jnp.where(right_half, corner_left, corner_right)
        made = mm(jnp.concatenate([here, side, across, corner], 1), w_mid[...])
        hidden = jnp.maximum(made + b_mid[0:1, :], 0.0).astype(kind)
        last = mm(w_last[...], hidden, ((1,), (1,)))
        for i in range(together):
            for k in range(MID_STEP):
                column = (i * MID_STEP + k) * 128
                c_ref[img + i, a + 1 + k] = last[:, column:column + 128]
        return carry

    if between is None:
        lax.fori_loop(0, images // together * steps, mid_layer, 0)
    else:
        lax.fori_loop(0, 1, mid_layer, 0)
        between()
        lax.fori_loop(1, images // together * steps, mid_layer, 0)

    lane = lax.broadcasted_iota(jnp.int32, (row_blocks * 8, 128), 1)
    sub = lax.broadcasted_iota(jnp.int32, (row_blocks * 8, 128), 0) % 8
    half_sub = sub[:row_blocks * 4]

    def moved(value):
        before = jnp.where(lane >= 16, pltpu.roll(value, 16, 1), jnp.where(lane >= 1, pltpu.roll(value, 17, 1), 0.0))
        after = jnp.where(lane < 112, pltpu.roll(value, 112, 1), jnp.where(lane < 127, pltpu.roll(value, 111, 1), 0.0))
        return jnp.where(sub < 4, before, after)

    for img in range(images):

        def piece(at, down=0):
            return c_ref[img, 1 + down:1 + down + row_blocks, at:at + 8, :].reshape(row_blocks * 8, 128)

        total = piece(0) + moved(piece(8))
        edges = piece(16) + moved(piece(24))
        c_ref[img, 1:1 + row_blocks, 16:24, :] = edges.reshape(row_blocks, 8, 128)
        total += jnp.where(sub % 4 == 0, piece(16, -1), 0.0) + jnp.where(sub % 4 == 3, piece(16, 1), 0.0)
        twos = total.reshape(row_blocks // 2, 16, 128)
        even = twos[:, 0:8].reshape(row_blocks * 4, 128)
        odd = twos[:, 8:16].reshape(row_blocks * 4, 128)
        left = jnp.where(half_sub < 4, even, pltpu.roll(odd, 4, 0))
        right_side = jnp.where(half_sub < 4, pltpu.roll(even, rows - 4, 0), odd)
        emit(img // frames, img % frames, mm(jnp.concatenate([left, right_side], 1).astype(kind), gather))


def built_shapes(frames):
    return [
        pltpu.VMEM((192, frames * 512), jnp.bfloat16),
        pltpu.VMEM((8, frames * 512), jnp.float32),
        pltpu.VMEM((768, 256), jnp.bfloat16),
        pltpu.VMEM((8, 256), jnp.float32),
        pltpu.VMEM((32, 256), jnp.bfloat16),
        pltpu.VMEM((32, 512), jnp.float32),
    ]


def work_shapes(pairs, frames, rows):
    images = pairs * frames
    return [
        pltpu.VMEM((pairs * 2, rows + 16, 512), jnp.float32),
        pltpu.VMEM((images, rows // 4 + 2, 160, 256), jnp.bfloat16),
        pltpu.VMEM((images, rows // 4 + 2, 32, 128), jnp.float32),
    ]


def filtered(source, response, cos, sin):
    kind = jnp.bfloat16
    row_real = mm(source, cos).astype(kind)
    row_imag = (-mm(source, sin)).astype(kind)
    gain = 1.0 / (1.0 + response)
    spec_real = ((mm(cos, row_real) + mm(sin, row_imag)) * gain).astype(kind)
    spec_imag = ((mm(cos, row_imag) - mm(sin, row_real)) * gain).astype(kind)
    back_real = (mm(cos, spec_real) - mm(sin, spec_imag)).astype(kind)
    back_imag = (mm(cos, spec_imag) + mm(sin, spec_real)).astype(kind)
    return (mm(back_real, cos) - mm(back_imag, sin)) * (1.0 / (source.shape[0] * source.shape[1]))


def whole_kernel(depth, states_at, measured_at, response_at, cosine_at, sines_at, *rest):
    params, tables, spread, gather = rest[:5], rest[5:7], rest[7], rest[8]
    data, z_res, x_res, y_res = rest[9:13]
    rest = rest[13:]
    built = [rest[0:6], rest[6:12], rest[12:18]]
    z_work, xy_work = rest[18:21], rest[21:24]
    z_own, z_other, turned, rows_f32 = rest[24:28]
    there, back = rest[28:31], rest[31:34]
    states, measured, response, cosine, sines, loaded = rest[34:40]
    z_send, z_recv = rest[40:42]
    there_sems, back_sems = rest[42:47], rest[47:52]
    kind = jnp.bfloat16
    devices = 2 * depth
    frame = lax.axis_index("frame")
    plane = lax.axis_index("plane")
    chips = devices // 2
    chip = (frame * depth + plane) // 2
    core = (frame * depth + plane) % 2
    sibling = (frame, plane + 1 - 2 * core)

    def at(k):
        other = (chip ^ k) * 2 + core
        return chip ^ k, (other // depth, other % depth)

    barrier = pltpu.get_barrier_semaphore()

    def greet(k, carry):
        pl.semaphore_signal(barrier, inc=1, device_id=at(k)[1], device_id_type=MESH)
        return carry

    loads = [pltpu.make_async_copy(states_at.at[k], states.at[k], loaded.at[k]) for k in range(4)]
    for k, (source, target) in enumerate(((measured_at, measured), (response_at, response), (cosine_at, cosine), (sines_at, sines))):
        loads.append(pltpu.make_async_copy(source, target, loaded.at[4 + k]))
    for k in (2, 3, 1, 0, 4, 5, 6, 7):
        loads[k].start()
    pl.semaphore_signal(barrier, inc=1, device_id=sibling, device_id_type=MESH)
    lax.fori_loop(1, chips, greet, 0, unroll=UNROLL)

    def pack(buffer):
        value = rows_f32[...].astype(kind).reshape(chips, 2, 8, 128)
        buffer[0] = value[:, 0]
        buffer[1] = value[:, 1]

    def unpack_rows(buffer):
        rows_f32[...] = buffer[...].astype(jnp.float32).reshape(devices * 8, 128)

    def within_chip(buffers, sems):
        source, mixed, _ = buffers
        keep, send, recv, _, _ = sems
        moves = [
            pltpu.make_async_copy(source.at[core], mixed.at[:, core], keep),
            pltpu.make_async_remote_copy(
                src_ref=source.at[1 - core], dst_ref=mixed.at[:, core], send_sem=send, recv_sem=recv,
                device_id=sibling, device_id_type=MESH,
            ),
        ]
        for move in moves:
            move.start()
        return moves

    loads[2].wait()
    loads[3].wait()
    for which, value in enumerate((jnp.transpose(states[2]), states[3])):
        for half in range(2):
            turned[which * 2 + half] = value[:, half * 128:(half + 1) * 128]
        for p in range(2):
            for half in range(2):
                rows_f32[pl.ds(which * 4 + p * 2 + half, devices, stride=8), :] = turned[which * 2 + half, pl.ds(p, devices, stride=2), :]
    pack(there[0])
    loads[1].wait()
    z_own[...] = states[1].astype(kind)
    pl.semaphore_wait(barrier, chips)

    def between_chips(buffers, sems, moves):
        _, mixed, target = buffers
        _, _, _, send, recv = sems
        for move in moves:
            move.wait()
        pltpu.make_async_copy(mixed.at[chip], target.at[chip], recv).start()

        def go(k, carry):
            other, coordinates = at(k)
            pltpu.make_async_remote_copy(
                src_ref=mixed.at[other], dst_ref=target.at[chip], send_sem=send, recv_sem=recv,
                device_id=coordinates, device_id_type=MESH,
            ).start()
            return carry

        lax.fori_loop(1, chips, go, 0, unroll=UNROLL)

    def finish(buffers, sems):
        _, mixed, target = buffers
        pltpu.make_async_copy(target, target, sems[4]).wait()
        some = mixed.at[pl.ds(0, chips - 1)]
        pltpu.make_async_copy(some, some, sems[3]).wait()

    there_moves = within_chip(there, there_sems)
    swap = pltpu.make_async_remote_copy(
        src_ref=z_own, dst_ref=z_other, send_sem=z_send, recv_sem=z_recv,
        device_id=(1 - frame, plane), device_id_type=MESH,
    )
    swap.start()
    prepare(0, params, tables, built[0], 1)
    prepare(1, params, tables, built[1], 2)
    between_chips(there, there_sems, there_moves)
    prepare(2, params, tables, built[2], 2)
    for k in (0, 4, 5, 6, 7):
        loads[k].wait()
    source = (measured[...] + states[0]).astype(kind)
    data[...] = filtered(source, response[...], cosine[...], sines[...])
    swap.wait()
    first_half([(lambda: z_own[...], lambda: z_other[...])], built[0], spread[...], *z_work, frames=1)

    finish(there, there_sems)
    unpack_rows(there[2])

    def rows_of(which, p, f, half):
        return pl.ds(f * depth * 8 + which * 4 + p * 2 + half, depth, stride=8)

    for which in range(2):

        def plane_of(p, f):
            return jnp.concatenate([rows_f32[rows_of(which, p, f, half), :] for half in range(2)], 1).astype(kind)

        def emit(p, f, value):
            for half in range(2):
                rows_f32[rows_of(which, p, f, half), :] = value[:, half * 128:(half + 1) * 128]

        pairs = [(functools.partial(plane_of, p, 0), functools.partial(plane_of, p, 1)) for p in range(2)]
        first_half(pairs, built[which + 1], spread[...], *xy_work, frames=2)
        second_half(built[which + 1], gather[...], emit, *xy_work[1:], frames=2)
    pack(back[0])
    back_moves = within_chip(back, back_sems)

    def emit_z(p, f, value):
        z_res[...] = value.astype(kind)

    second_half(built[0], gather[...], emit_z, *z_work[1:], frames=1, between=lambda: between_chips(back, back_sems, back_moves))
    finish(back, back_sems)
    unpack_rows(back[2])

    def unpack(which):
        for p in range(2):
            for half in range(2):
                turned[which * 2 + half, pl.ds(p, devices, stride=2), :] = rows_f32[pl.ds(which * 4 + p * 2 + half, devices, stride=8), :]
        return jnp.concatenate([turned[which * 2], turned[which * 2 + 1]], 1)

    x_res[...] = jnp.transpose(unpack(0)).astype(kind)
    y_res[...] = unpack(1).astype(kind)


def final_kernel(states, data, res_z, res_x, res_y, out):
    w = [states[k] for k in range(4)]
    z = [2.0 * data[...] - w[0]]
    z += [w[k + 1] - 2.0 * res[...].astype(jnp.float32) for k, res in enumerate((res_z, res_x, res_y))]
    twice = 0.5 * (z[0] + z[1] + z[2] + z[3])
    for k in range(4):
        out[k] = (1.0 - relaxation) * w[k] + relaxation * (twice - z[k])


def fourier_tables(length):
    indices = np.arange(length, dtype=np.int32)
    phase = indices[:, None] * indices[None, :] % length
    angle = phase.astype(np.float32) * np.float32(2.0 * math.pi / length)
    return (jnp.asarray(np.cos(angle), jnp.bfloat16), jnp.asarray(np.sin(angle), jnp.bfloat16))


def constants(width):
    kind = jnp.bfloat16
    tables = (first_table(), last_table(), spread_table(width), gather_table(width))
    return tuple(jnp.asarray(table.astype(kind)) for table in tables)


def on_device(states, measured, response, kernel_in, bias_in, kernel_mid, bias_mid, kernel_out):
    current = states[:, 0, 0]
    width = current.shape[-1]
    depth = lax.axis_size("plane")
    kind = jnp.bfloat16
    args = (current, measured[0, 0], response) + fourier_tables(width)
    args += (jnp.transpose(kernel_in, (0, 1, 3, 2)), bias_in, kernel_mid, bias_mid, jnp.transpose(kernel_out, (1, 0, 2))) + constants(width)
    short = pltpu.VMEM((width, width), kind)
    image = pltpu.VMEM((width, width), jnp.float32)
    by_core = pltpu.VMEM((2, depth, 8, 128), kind)
    by_chip = pltpu.VMEM((depth, 2, 8, 128), kind)
    sharp = jax.ShapeDtypeStruct((width, width), jnp.float32)
    coarse = jax.ShapeDtypeStruct((width, width), kind)
    found = pl.pallas_call(
        functools.partial(whole_kernel, depth),
        out_shape=(sharp, coarse, coarse, coarse),
        in_specs=[pl.BlockSpec(memory_space=pl.ANY)] * 5 + [pl.BlockSpec(memory_space=pltpu.VMEM)] * (len(args) - 5),
        out_specs=(pl.BlockSpec(memory_space=pltpu.VMEM),) * 4,
        scratch_shapes=built_shapes(1) + built_shapes(2) + built_shapes(2)
        + work_shapes(1, 1, width) + work_shapes(2, 2, depth)
        + [short, short, pltpu.VMEM((4, width, 128), jnp.float32), pltpu.VMEM((2 * depth * 8, 128), jnp.float32)]
        + [by_core, by_chip, by_chip] * 2
        + [pltpu.VMEM((4, width, width), jnp.float32), image, image, short, short, pltpu.SemaphoreType.DMA((8,))]
        + [pltpu.SemaphoreType.DMA] * 12,
        compiler_params=pltpu.CompilerParams(vmem_limit_bytes=60 * 2**20, collective_id=0, has_side_effects=True),
        cost_estimate=pl.CostEstimate(flops=12 * 10**9, bytes_accessed=2**22, transcendentals=0),
    )(*args)
    step = width // 2
    flat = pl.BlockSpec((step, width), lambda i: (i, 0))
    deep = pl.BlockSpec((4, step, width), lambda i: (0, i, 0))
    out = pl.pallas_call(
        final_kernel,
        grid=(2,),
        out_shape=jax.ShapeDtypeStruct(current.shape, jnp.float32),
        in_specs=[deep, flat, flat, flat, flat],
        out_specs=deep,
        cost_estimate=pl.CostEstimate(flops=2 * 10**6, bytes_accessed=2**21, transcendentals=0),
    )(current, *found)
    return out[:, None, None]


def solution(mesh):
    placed = (
        P(None, "frame", "plane", None, None),
        P("frame", "plane", None, None),
        P(),
        P(),
        P(),
        P(),
        P(),
        P(),
    )
    return jax.shard_map(
        on_device,
        mesh=mesh,
        in_specs=placed,
        out_specs=P(None, "frame", "plane", None, None),
        check_vma=False,
    )
```
